256 devices in a mesh: dp: 32 (over x, y, core), mp: 8 (over z).
Axes of the slice: x: 4, y: 4, z: 8, core: 2. Of those that a mesh axis runs over, the one named last changes fastest.
Arguments:
- residual: bfloat16 [4096, 4096], P('dp', 'mp'), may hold values from -6 to 6
- queries: bfloat16 [4096, 4096], P('dp', 'mp'), may hold values from -36 to 36
- key_rows: bfloat16 [4096, 4096], P('dp', 'mp'), may hold values from -36 to 36
- value_rows: bfloat16 [4096, 4096], P('dp', 'mp'), may hold values from -6 to 6
- lengths: int32 [32, 4], P('dp'), may hold values from 1 to 64, 128 in all within a row
- labels: int32 [4096, 1], P('dp'), may hold values from 0 to 7; in each aligned block of 128 rows (0 to 127, 128 to 255, ...) at most 24 rows name the same one
- losses: float32 [4096], P('dp'), may hold values from 1 to 30, as said below
- prior_weights: float32 [8], replicated, may hold values from 0.05 to 0.5
- norm_gain: float32 [4096], replicated, may hold values from 0.1 to 1.9
- gate_weight: bfloat16 [4096, 88064], P(None, ('dp', 'mp')), may hold values from -0.09375 to 0.09375
- up_weight: bfloat16 [4096, 88064], P(None, ('dp', 'mp')), may hold values from -0.09375 to 0.09375
- down_weight: bfloat16 [88064, 4096], P(('dp', 'mp')), may hold values from -0.25 to 0.25
Outputs:
- mixed: bfloat16 [4096, 4096], P('dp', 'mp')
- relative_weights: float32 [8], replicated
The draws below stay inside these ranges and needn't reach their ends.
Inputs may be any that keep to these rules, and one draw needn't show every extreme that they name: `labels`: in each packed sequence no label is carried by more than 24 tokens, and in every draw some sequence has exactly 24 tokens of one label; every label occurs somewhere. `losses`: Positive.
All inputs are finite; a program needn't handle non-finite values.
Results may differ from the reference program's by a relative error of at most 0.014.
Values may be sent and summed in bfloat16 or wider, within the bound.
A program may use at most 128 MiB of HBM per device.

```python
import math
import jax
import jax.numpy as jnp
import numpy as np
from jax import lax

D = 4096
FF = 11008
HEAD_DIM = 128
EXPERTS = 8
TOK_DEV = 128
DOCS = 4
CAP = 24
ROWS = 32
TOKENS = 4096
N_DP = 32


def draw_queries(key, part):
    key = jax.random.fold_in(key, 11)
    fresh = jnp.clip(jax.random.normal(key, (TOKENS, D), jnp.float32), -6.0, 6.0)
    return fresh.astype(jnp.bfloat16)


def draw_key_rows(key, part):
    key = jax.random.fold_in(key, 12)
    fresh = jnp.clip(jax.random.normal(key, (TOKENS, D), jnp.float32), -6.0, 6.0)
    return fresh.astype(jnp.bfloat16)


def draw_losses(key, part):
    key = jax.random.fold_in(key, 21)
    positions = jnp.arange(TOKENS, dtype=jnp.float32)
    ramp = 1.0 + 2.0 * positions / max(TOKENS - 1, 1)
    base = jnp.exp(jax.random.uniform(key, (TOKENS,), jnp.float32, 0.0, math.log(10.0)))
    return base * ramp


def with_spikes(array, key, source, target, parts, factor):
    def block_of(dim):
        return (jnp.arange(array.shape[dim]) // (array.shape[dim] // parts)).reshape((-1,) + (1,) * (array.ndim - 1 - dim))

    near = jax.random.permutation(key, parts)[block_of(target)]
    other_side = (block_of(target) + parts // 2) % parts
    return jnp.where((block_of(source) == near) | (block_of(source) == other_side), factor * array, array)


def shard_levels(key, dims, cuts, least, high):
    factor_of, own = 1.0, jax.random.fold_in(key, 6)
    for position, parts in cuts:
        heights = jnp.exp(jax.random.uniform(jax.random.fold_in(own, position), (parts,), jnp.float32, least / len(cuts), high / len(cuts)))
        factor_of = factor_of * jnp.repeat(heights, dims[position] // parts).reshape([-1 if axis == position else 1 for axis in range(len(dims))])
    return factor_of


def length_profile(number_of, total, bound, lean):
    loads = [(1 << 20) // math.isqrt(grade ** lean) + 1 for grade in range(2, number_of + 1)]
    rest, given = total - bound - (number_of - 1), [1] * (number_of - 1)
    while rest > 0:
        candidates = [i for i in range(number_of - 1) if given[i] < bound]
        whole, remaining = sum([loads[i] for i in candidates]), rest
        for i in candidates:
            addition = min(bound - given[i], max(1, remaining * loads[i] // whole), rest)
            given[i] = given[i] + addition
            rest = rest - addition
    return np.array([bound] + given)


def uneven_parts(rng, amount, total, bound, lean):
    if amount == 2:
        one = jax.random.randint(rng, (), max(1, total - bound), min(bound, total - 1) + 1)
        return jnp.stack([one, total - one])
    sizes = jnp.asarray(length_profile(amount, total, bound, lean), jnp.int32)
    couples = (amount - 1) // 2
    giver, sink = sizes[1:1 + 2 * couples:2], sizes[2:2 + 2 * couples:2]
    slack = jnp.minimum(giver - 1, bound - sink)
    shifted = jax.random.randint(jax.random.fold_in(rng, 1), (couples,), 0, 1 << 20) % (slack + 1)
    sizes = sizes.at[1:1 + 2 * couples:2].set(giver - shifted).at[2:2 + 2 * couples:2].set(sink + shifted)
    return sizes[jax.random.permutation(jax.random.fold_in(rng, 2), amount)]


def shared_out(stream_key, own, number, rows, count, top, bound, lean):
    ranking = jax.random.permutation(stream_key, count)
    packed, common = shares(count, rows * top, bound, lean, True), shares(count, rows * top, bound, lean, False)
    places = jnp.arange(count)

    def named(sizes, offset_by):
        used = int((sizes > 0).sum())
        fixed = max(1, used // 4)
        moved = fixed + (places - fixed + offset_by * (used - fixed)) % max(1, count - fixed)
        return jnp.zeros((count,), jnp.int32).at[ranking[jnp.where(places < fixed, places, moved)]].set(jnp.asarray(sizes, jnp.int32))

    sizes = jnp.where(number % 4 == 0, named(packed, number // 4), named(common, number - number // 4 - 1))
    mixed = jax.random.permutation(jax.random.fold_in(own, 3), count)
    source_of, receiver = mixed[0:count // 2 * 2:2], mixed[1:count // 2 * 2:2]
    margin = jnp.minimum(sizes[source_of] - 1, bound - sizes[receiver]) // 2
    margin = jnp.where((source_of == ranking[0]) | (receiver == ranking[0]) | (sizes[receiver] == 0), 0, jnp.maximum(margin, 0))
    moved = jax.random.randint(jax.random.fold_in(own, 4), (count // 2,), 0, 1 << 20) % (margin + 1)
    sizes = sizes.at[source_of].add(-moved).at[receiver].add(moved)
    items = jnp.searchsorted(jnp.cumsum(sizes), jnp.arange(rows * top), side="right").astype(jnp.int32)
    table = items.reshape(top, rows).T
    table = table[jax.random.permutation(jax.random.fold_in(own, 1), rows)]
    offset_by = jax.random.randint(jax.random.fold_in(own, 2), (rows, 1), 0, top)
    return jnp.take_along_axis(table, (jnp.arange(top)[None, :] + offset_by) % top, axis=1)


def shares(number_of, total, most, skew, full):
    portions = [(1 << 20) // math.isqrt(rank ** skew) + 1 for rank in range(1, number_of + 1)]
    largest = most if full else min(most, max(-(-total // number_of), total * portions[0] // sum(portions)))
    least = 1 if total - largest >= number_of - 1 else 0
    given, rest = [largest] + [least] * (number_of - 1), total - largest - least * (number_of - 1)
    while rest > 0:
        movable = [i for i in range(1, number_of) if given[i] < largest] or [i for i in range(1, number_of) if given[i] < most]
        whole, budget = sum([portions[i] for i in movable]), rest
        for i in movable:
            more = min(most - given[i], max(1, budget * portions[i] // whole), rest)
            given[i] = given[i] + more
            rest = rest - more
    return np.array(given)


def scatter_about(own_key, dims, width, reach, shards=(), held_as=jnp.bfloat16):
    entries = jax.random.normal(own_key, dims, jnp.float32) * width
    if len(shards) > 0:
        entries = shard_levels(own_key, dims, shards, -0.22, 0.18) * entries
    return jnp.clip(entries, min=-reach, max=reach).astype(held_as)


def noise_with(stream_key, extent, scale, reach, pieces, heavy, kind=jnp.bfloat16):
    array = scale * jax.random.normal(stream_key, extent, jnp.float32)
    if pieces:
        array = array * shard_levels(stream_key, extent, pieces, -0.22, 0.18)
    return jnp.clip(with_spikes(array, jax.random.fold_in(stream_key, 3), *heavy), -reach, reach).astype(kind)


def setup_inputs(seed: int = 0) -> dict:
    key_list = jax.random.split(jax.random.key(seed), 13)
    residual = scatter_about(key_list[0], (TOKENS, D), 1.0, 6.0, ((0, 32), (1, 8)))
    queries = draw_queries(jax.random.fold_in(key_list[12], 71), 0)
    key_rows = draw_key_rows(jax.random.fold_in(key_list[12], 71), 0)
    value_rows = scatter_about(key_list[3], (TOKENS, D), 1.0, 6.0, ((0, 32), (1, 8)))
    lengths = jax.vmap(lambda own: uneven_parts(own, DOCS, TOK_DEV, TOK_DEV // 2, 2))(jax.random.split(key_list[4], ROWS)).reshape((ROWS, DOCS)).astype(jnp.int32)
    labels_keys = jax.random.split(jax.random.fold_in(key_list[5], 1), TOKENS // TOK_DEV)
    labels_turns = jax.random.permutation(jax.random.fold_in(key_list[5], 3), TOKENS // TOK_DEV)
    labels = jax.vmap(lambda own, number: shared_out(jax.random.fold_in(key_list[5], 2), own, number, TOK_DEV, EXPERTS, 1, CAP, 1))(labels_keys, labels_turns).reshape((TOKENS, 1))
    losses = draw_losses(jax.random.fold_in(key_list[12], 71), 0)
    prior_weights = jnp.clip(jnp.exp(jax.random.uniform(key_list[7], (EXPERTS,), jnp.float32, math.log(0.05), math.log(0.5))), 0.05, 0.5)
    norm_gain = jnp.clip(1.0 + 0.18 * jax.random.normal(key_list[8], (D,), jnp.float32), 0.1, 1.9)
    gate_weight = scatter_about(key_list[9], (D, EXPERTS * FF), D ** -0.5, 0.09375, ((1, 256),))
    up_weight = scatter_about(key_list[10], (D, EXPERTS * FF), D ** -0.5, 0.09375, ((1, 256),))
    down_weight = noise_with(key_list[11], (EXPERTS * FF, D), FF ** -0.5, 0.25, ((0, 256),), (0, 1, 256, 6.0))
    return dict(residual=residual, queries=queries, key_rows=key_rows, value_rows=value_rows, lengths=lengths, labels=labels, losses=losses, prior_weights=prior_weights, norm_gain=norm_gain, gate_weight=gate_weight, up_weight=up_weight, down_weight=down_weight)


dro_step = 0.5

def attend(queries, key_rows, value_rows, doc_lengths):
    seq_len = queries.shape[0]
    positions = jnp.arange(seq_len, dtype=jnp.int32)
    doc_ends = jnp.cumsum(doc_lengths.astype(jnp.int32)).astype(jnp.int32)
    doc_ids = lax.optimization_barrier(jnp.sum((positions[:, None] >= doc_ends[None, :]).astype(jnp.int32), axis=1))
    allowed = (doc_ids[:, None] == doc_ids[None, :]) & (positions[None, :] <= positions[:, None])
    q_heads = queries.reshape(seq_len, -1, HEAD_DIM).astype(jnp.float32)
    k_heads = key_rows.reshape(seq_len, -1, HEAD_DIM).astype(jnp.float32)
    v_heads = value_rows.reshape(seq_len, -1, HEAD_DIM).astype(jnp.float32)
    scores = jnp.einsum('qhd,khd->hqk', q_heads, k_heads) * HEAD_DIM ** (-0.5)
    scores = jnp.where(allowed[None], scores, -1e+30)
    row_max = lax.optimization_barrier(jnp.max(scores, axis=-1, keepdims=True))
    exp_scores = jnp.exp(scores - row_max)
    attn_probs = (exp_scores / lax.optimization_barrier(jnp.sum(exp_scores, axis=-1, keepdims=True))).astype(jnp.bfloat16)
    attn_probs = lax.optimization_barrier(attn_probs)
    attn = jnp.einsum('hqk,khd->qhd', attn_probs.astype(jnp.float32), v_heads)
    return attn.reshape(seq_len, -1)

def reference(residual, queries, key_rows, value_rows, lengths, labels, losses, prior_weights, norm_gain, gate_weight, up_weight, down_weight):

    def one_sequence(pack):
        return attend(pack[0], pack[1], pack[2], pack[3])
    attn = lax.map(one_sequence, (queries.reshape(N_DP, TOK_DEV, D), key_rows.reshape(N_DP, TOK_DEV, D), value_rows.reshape(N_DP, TOK_DEV, D), lengths)).reshape(TOKENS, D)
    hidden_state = (residual.astype(jnp.float32) + attn).astype(jnp.bfloat16)
    hidden_float = hidden_state.astype(jnp.float32)
    scale_rows = lax.rsqrt(lax.optimization_barrier(jnp.mean(hidden_float * hidden_float, axis=1, keepdims=True)) + 1e-05)
    normed = (hidden_float * scale_rows * norm_gain[None, :]).astype(jnp.bfloat16)
    token_labels = labels[:, 0].astype(jnp.int32)
    onehot_int = (token_labels[:, None] == jnp.arange(EXPERTS, dtype=jnp.int32)[None, :]).astype(jnp.int32)
    seq_onehot = onehot_int.reshape(N_DP, TOK_DEV, EXPERTS)
    before = (jnp.cumsum(seq_onehot, axis=1) - seq_onehot).astype(jnp.int32)
    slot_rank = lax.optimization_barrier(jnp.sum(before * seq_onehot, axis=2)).reshape(TOKENS).astype(jnp.int32)
    seq_index = (jnp.arange(TOKENS, dtype=jnp.int32) // TOK_DEV).astype(jnp.int32)
    slot_total = N_DP * CAP
    destination = (token_labels * slot_total + seq_index * CAP + slot_rank).astype(jnp.int32)
    buffer = jnp.zeros((EXPERTS * slot_total, D), jnp.bfloat16).at[destination].set(normed)
    buffer = buffer.reshape(EXPERTS, slot_total, D)

    def run_expert(pack):
        expert, expert_rows = pack
        start = (expert * FF).astype(jnp.int32)
        w_gate = lax.dynamic_slice_in_dim(gate_weight, start, FF, 1)
        w_up = lax.dynamic_slice_in_dim(up_weight, start, FF, 1)
        w_down = lax.dynamic_slice_in_dim(down_weight, start, FF, 0)
        gate_act = jnp.dot(expert_rows, w_gate, preferred_element_type=jnp.float32)
        up_act = jnp.dot(expert_rows, w_up, preferred_element_type=jnp.float32)
        inner_act = (jax.nn.silu(gate_act) * up_act).astype(jnp.bfloat16)
        return jnp.dot(inner_act, w_down, preferred_element_type=jnp.float32)
    results = lax.map(run_expert, (jnp.arange(EXPERTS, dtype=jnp.int32), buffer)).reshape(EXPERTS * slot_total, D)
    expert_out = results[destination]
    mixed = (hidden_float + expert_out).astype(jnp.bfloat16)
    onehot = onehot_int.astype(jnp.float32)
    loss_total = lax.optimization_barrier(jnp.sum(onehot * losses[:, None], axis=0))
    token_count = lax.optimization_barrier(jnp.sum(onehot, axis=0))
    domain_mean = loss_total / token_count
    scaled = prior_weights * jnp.exp(dro_step * domain_mean)
    relative_weights = EXPERTS * scaled / jnp.sum(scaled)
    return (mixed, relative_weights)
```

```python
import jax
import jax.numpy as jnp
from jax import lax
from jax.experimental import pallas as pl
from jax.experimental.pallas import tpu as pltpu
from jax.sharding import PartitionSpec as P

HEAD_DIM = 128
EXPERTS = 8
CAP = 24
PAD = 32
TOK = 128
COLS = 512
HID = 344
NZ = 8
CORE_ROWS = 16 * CAP
ROWS = 2 * CORE_ROWS
CHUNK = 4 * CAP
SHARED = 2 * CHUNK
RIGHT, LEFT = 0, 1
F32, BF16 = jnp.float32, jnp.bfloat16
MESH = pl.DeviceIdType.MESH

dro_step = 0.5


def kernel(
    lengths_ref, labels_ref, losses_ref, prior_ref, gain_ref,
    res_hbm, q_hbm, k_hbm, v_hbm, gate_hbm, up_hbm, down_hbm,
    mixed_ref, weights_ref,
    res_v, q_v, k_v, v_v, gate_v, up_v, down_v,
    hidden, packed, stage, xb, acc_g, acc_u, square, inner,
    part, sib_out, sib_in, ring_in, ring_out, y_out, y_in, ret_out, ret,
    stat_x, stat_y, stat_c, stat_src,
    in_sem, w_sem, a_send, a_recv, g_send, g_recv, gs_send, gs_recv, gy_send, gy_recv,
    rs_send, rs_recv, ry_send, ry_recv, r_send, r_recv, b_send, b_recv, st_send, st_recv,
):
    dp = lax.axis_index("dp")
    z = lax.axis_index("mp")
    core = lax.rem(dp, 2)
    xy = dp // 2
    x, y = xy // 4, lax.rem(xy, 4)
    yb = lax.rem(y, 2)

    def plane(tx, ty, tc=None):
        return ((tx * 4 + ty) * 2 + (core if tc is None else tc), z)

    sibling = (dp + 1 - 2 * core, z)
    partner = plane(x, y + 1 - 2 * yb)
    z_right = (dp, lax.rem(z + 1, NZ))
    z_left = (dp, lax.rem(z + NZ - 1, NZ))
    toward = (z_right, z_left)
    offsets = [((i // 4), i % 4) for i in range(1, 16)]

    barrier = pltpu.get_barrier_semaphore()
    peers = [plane(lax.rem(x + dx, 4), lax.rem(y + dy, 4)) for dx, dy in offsets]
    peers += [sibling, z_right, z_left]
    for peer in peers:
        pl.semaphore_signal(barrier, inc=1, device_id=peer, device_id_type=MESH)

    loads = [
        pltpu.make_async_copy(src, dst, in_sem.at[i])
        for i, (src, dst) in enumerate(((q_hbm, q_v), (k_hbm, k_v), (v_hbm, v_v), (res_hbm, res_v)))
    ]
    for load in loads:
        load.start()
    weight_loads = [
        pltpu.make_async_copy(gate_hbm, gate_v, w_sem.at[0]),
        pltpu.make_async_copy(up_hbm, up_v, w_sem.at[1]),
    ] + [
        pltpu.make_async_copy(down_hbm.at[:, pl.ds(i * COLS, COLS)], down_v.at[i], w_sem.at[2 + i])
        for i in range(NZ)
    ]
    for load in weight_loads:
        load.start()

    def remote(src, dst, send, recv, device):
        return pltpu.make_async_remote_copy(
            src_ref=src, dst_ref=dst, send_sem=send, recv_sem=recv,
            device_id=device, device_id_type=MESH,
        )

    at0 = lax.broadcasted_iota(jnp.int32, (TOK, TOK), 0)
    at1 = lax.broadcasted_iota(jnp.int32, (TOK, TOK), 1)
    label_col = labels_ref[...].astype(F32)
    label_row = jnp.sum(jnp.where(at0 == at1, label_col, 0.0), axis=0, keepdims=True)
    same = label_col == label_row
    rank_row = jnp.sum(jnp.where(same & (at0 < at1), 1.0, 0.0), axis=0, keepdims=True)
    rank_col = jnp.sum(jnp.where(same & (at1 < at0), 1.0, 0.0), axis=1, keepdims=True)
    slot_row = label_row * PAD + rank_row
    slot_ids = lax.broadcasted_iota(jnp.int32, (EXPERTS * PAD, TOK), 0).astype(F32)
    select = (slot_ids == slot_row).astype(BF16)

    domain = lax.broadcasted_iota(jnp.int32, (EXPERTS, TOK), 0).astype(F32)
    lane = lax.broadcasted_iota(jnp.int32, (EXPERTS, TOK), 1)
    member = (domain == label_row).astype(F32)
    loss_sum = jnp.sum(member * losses_ref[...], axis=1, keepdims=True)
    count = jnp.sum(member, axis=1, keepdims=True)
    stat_src[0] = jnp.where(lane == 0, loss_sum, jnp.where(lane == 1, count, 0.0))

    ends = [lengths_ref[0, 0]]
    for i in range(1, 4):
        ends.append(ends[-1] + lengths_ref[0, i])
    doc0 = sum((at0 >= end).astype(jnp.int32) for end in ends)
    doc1 = sum((at1 >= end).astype(jnp.int32) for end in ends)
    allowed = (doc0 == doc1) & (at1 <= at0)
    for load in loads:
        load.wait()
    for head in range(COLS // HEAD_DIM):
        cut = slice(head * HEAD_DIM, (head + 1) * HEAD_DIM)
        scores = lax.dot_general(
            q_v[:, cut], k_v[:, cut], (((1,), (1,)), ((), ())), preferred_element_type=F32
        ) * HEAD_DIM ** (-0.5)
        scores = jnp.where(allowed, scores, -1e30)
        exp_scores = jnp.exp(scores - jnp.max(scores, axis=1, keepdims=True))
        probs = (exp_scores / jnp.sum(exp_scores, axis=1, keepdims=True)).astype(BF16)
        attn = jnp.dot(probs, v_v[:, cut], preferred_element_type=F32)
        hidden[:, cut] = (res_v[:, cut].astype(F32) + attn).astype(BF16)
    packed[...] = (
        jnp.dot(select, hidden[...], preferred_element_type=F32)
        .astype(BF16)
        .reshape(EXPERTS, PAD, COLS)
    )

    pl.semaphore_wait(barrier, len(peers))

    my_q = jnp.where(x >= 2, (x - 2) * 4 + y, 8 + y)

    def goes(ty):
        return (x >= 2) | (lax.rem(ty, 2) == x)

    def send_block(i):
        dx, dy = offsets[i]
        tx, ty = lax.rem(x + dx, 4), lax.rem(y + dy, 4)
        copy = remote(
            packed.at[2 * tx + ty // 2], stage.at[my_q], a_send.at[i], a_recv.at[my_q], plane(tx, ty)
        )
        return goes(ty), copy

    for i in range(15):
        allowed_i, copy = send_block(i)
        pl.when(allowed_i)(copy.start)

    @pl.when(goes(y))
    def _():
        stage[my_q] = packed[2 * x + y // 2]

    def seq_of(q):
        if q < 8:
            return 2 + q // 4, q % 4
        return yb, q - 8

    def stat_copy(i, phase):
        if phase == 0:
            dst, peer = stat_x, plane(lax.rem(x + i, 4), y)
            return remote(stat_src.at[0], dst.at[x], st_send.at[i - 1], st_recv.at[x], peer)
        if phase == 1:
            dst, peer = stat_y, plane(x, lax.rem(y + i, 4))
            return remote(stat_src.at[1], dst.at[y], st_send.at[2 + i], st_recv.at[4 + y], peer)
        return remote(stat_src.at[2], stat_c, st_send.at[6], st_recv.at[8], sibling)

    def stat_wait(i, phase):
        if phase == 0:
            at = lax.rem(x + i, 4)
            return remote(stat_src.at[0], stat_x.at[at], st_send.at[0], st_recv.at[at], plane(at, y))
        at = lax.rem(y + i, 4)
        return remote(stat_src.at[1], stat_y.at[at], st_send.at[0], st_recv.at[4 + at], plane(x, at))

    for i in range(1, 4):
        stat_copy(i, 0).start()
    stat_x[x] = stat_src[0]

    base = core * CORE_ROWS
    sib_base = (1 - core) * CORE_ROWS
    own_off = SHARED + yb * CHUNK
    other_off = SHARED + (1 - yb) * CHUNK
    OWN, C0, C1, OTHER = 0, 1, 2, 3
    piece_off = (own_off, 0, CHUNK, other_off)

    def slice_at(rel):
        return lax.rem(z + rel, NZ)

    def block(rel, off, rows):
        start = pl.multiple_of(base + off, 16)
        return xb.at[slice_at(rel), pl.ds(start, rows)]

    def gather_copy(way, hop, piece, sending, off=None, rows=CHUNK):
        sign = 1 if way == LEFT else -1
        behind = hop - 1 if sending else hop
        rel = (sign * behind) % NZ
        ref = block(rel, piece_off[piece] if off is None else off, rows)
        return remote(
            ref, ref, g_send.at[way, hop - 1, piece], g_recv.at[way, hop - 1, piece], toward[way]
        )

    HALF = CHUNK // 2
    far = {
        (RIGHT, OWN): dict(off=own_off, rows=CHUNK),
        (RIGHT, C0): dict(off=0, rows=HALF),
        (LEFT, C0): dict(off=HALF, rows=HALF),
        (LEFT, C1): dict(off=CHUNK, rows=CHUNK),
    }

    def sib_copy(rel, piece, mine=True):
        start = pl.multiple_of((base if mine else sib_base) + piece_off[piece], 16)
        ref = xb.at[slice_at(rel), pl.ds(start, CHUNK)]
        return remote(ref, ref, gs_send.at[rel, piece], gs_recv.at[rel, piece], sibling)

    def y_copy(rel, mine=True):
        ref = block(rel, own_off if mine else other_off, CHUNK)
        return remote(ref, ref, gy_send.at[rel], gy_recv.at[rel], partner)

    started = []

    def go(copy):
        copy.start()
        started.append(copy)

    def spread(rel, piece):
        if piece == OWN:
            go(y_copy(rel))
        go(sib_copy(rel, piece))

    for piece, first in ((OWN, 8), (C0, 0), (C1, 4)):
        for q in range(first, first + 4):
            sx, sy = seq_of(q)
            arrival = remote(
                packed.at[0], stage.at[q], a_send.at[0], a_recv.at[q], plane(sx, sy)
            )
            pl.when((sx != x) | (sy != y))(arrival.wait_recv)
        rows = stage[first:first + 4].astype(F32)[:, :CAP].reshape(CHUNK, COLS).astype(BF16)
        start = pl.multiple_of(base + piece_off[piece], 16)
        xb[z, pl.ds(start, CHUNK)] = rows
        go(gather_copy(RIGHT, 1, piece, True))
        go(gather_copy(LEFT, 1, piece, True))
        spread(0, piece)

    for ref in (acc_g, acc_u, square):
        ref[...] = jnp.zeros_like(ref)

    BLOCK = SHARED

    def multiply(rels, rows_from):
        def one(i, carry):
            rel = rels[0] if len(rels) == 1 else jnp.where(i == 0, rels[0], rels[1])
            s = slice_at(rel)
            at = pl.multiple_of(s * COLS, COLS)
            gain = gain_ref[pl.ds(s, 1), :]
            for start in rows_from:
                here = pl.ds(pl.multiple_of(start, 16), BLOCK)
                value = xb[s, here, :].astype(F32)
                sq = value * value
                square[here, :] += (
                    sq[:, :128] + sq[:, 128:256] + sq[:, 256:384] + sq[:, 384:]
                )
                scaled = (value * gain).astype(BF16)
                acc_g[here, :] += jnp.dot(
                    scaled, gate_v[pl.ds(at, COLS), :], preferred_element_type=F32
                )
                acc_u[here, :] += jnp.dot(
                    scaled, up_v[pl.ds(at, COLS), :], preferred_element_type=F32
                )
            return carry

        lax.fori_loop(0, len(rels), one, 0)

    def settle(rels, j):
        if j == 0:
            for rel in rels:
                y_copy(rel, mine=False).wait_recv()
                go(sib_copy(rel, OTHER))
            multiply(rels, (base,))
        elif j == 1:
            for rel in rels:
                sib_copy(rel, C0, mine=False).wait_recv()
                sib_copy(rel, C1, mine=False).wait_recv()
            multiply(rels, (sib_base,))
        else:
            for rel in rels:
                sib_copy(rel, OWN, mine=False).wait_recv()
                sib_copy(rel, OTHER, mine=False).wait_recv()
            multiply(rels, (base + SHARED, sib_base + SHARED))

    weight_loads[0].wait()
    weight_loads[1].wait()
    before = (0,)
    for hop in (1, 2, 3):
        for j, piece in enumerate((OWN, C0, C1)):
            for way in (RIGHT, LEFT):
                gather_copy(way, hop, piece, False).wait_recv()
                if hop < 3:
                    go(gather_copy(way, hop + 1, piece, True))
                elif (way, piece) in far:
                    go(gather_copy(way, 4, piece, True, **far[way, piece]))
                spread(hop if way == LEFT else NZ - hop, piece)
            settle(before, j)
        before = (hop, NZ - hop)
        if hop == 1:
            for i in range(1, 4):
                stat_wait(i, 0).wait_recv()
            stat_src[1] = (stat_x[0] + stat_x[1]) + (stat_x[2] + stat_x[3])
            for i in range(1, 4):
                stat_copy(i, 1).start()
            stat_y[y] = stat_src[1]
        if hop == 2:
            for i in range(1, 4):
                stat_wait(i, 1).wait_recv()
            stat_src[2] = (stat_y[0] + stat_y[1]) + (stat_y[2] + stat_y[3])
            stat_copy(0, 2).start()
    gather_copy(RIGHT, 4, OWN, False, **far[RIGHT, OWN]).wait_recv()
    spread(4, OWN)
    settle(before, 0)
    gather_copy(RIGHT, 4, C0, False, **far[RIGHT, C0]).wait_recv()
    gather_copy(LEFT, 4, C0, False, **far[LEFT, C0]).wait_recv()
    spread(4, C0)
    settle(before, 1)
    gather_copy(LEFT, 4, C1, False, **far[LEFT, C1]).wait_recv()
    spread(4, C1)
    settle(before, 2)
    for j in range(3):
        settle((4,), j)

    def activate(i, carry):
        here = pl.ds(pl.multiple_of(i * BLOCK, BLOCK), BLOCK)
        mean = jnp.sum(square[here, :], axis=1, keepdims=True) * (1.0 / (NZ * COLS))
        scale = lax.rsqrt(mean + 1e-05)
        gate = acc_g[here, :] * scale
        up = acc_u[here, :] * scale
        inner[here, :] = (gate / (1.0 + jnp.exp(-gate)) * up).astype(BF16)
        return carry

    lax.fori_loop(0, ROWS // BLOCK, activate, 0)
    for load in weight_loads[2:]:
        load.wait()

    def rs_copy(rel):
        return remote(
            sib_out.at[rel], sib_in.at[rel], rs_send.at[rel], rs_recv.at[rel], sibling
        )

    def ry_copy(rel):
        return remote(y_out.at[rel], y_in.at[rel], ry_send.at[rel], ry_recv.at[rel], partner)

    def prepare(rel):
        weight = down_v.at[slice_at(rel)]

        def one(i, carry):
            off = pl.multiple_of(i * BLOCK, BLOCK)
            theirs = inner[pl.ds(pl.multiple_of(sib_base + off, 16), BLOCK), :]
            sib_out[rel, pl.ds(off, BLOCK)] = jnp.dot(
                theirs, weight[...], preferred_element_type=F32
            ).astype(BF16)
            return carry

        lax.fori_loop(0, 2, one, 0)
        go(rs_copy(rel))

        def two(i, carry):
            off = pl.multiple_of(i * BLOCK, BLOCK)
            mine = inner[pl.ds(pl.multiple_of(base + off, 16), BLOCK), :]
            part[rel, pl.ds(off, BLOCK)] = jnp.dot(mine, weight[...], preferred_element_type=F32)
            return carry

        lax.fori_loop(0, 2, two, 0)

    def join(rel):
        rs_copy(rel).wait_recv()
        other = pl.ds(pl.multiple_of(other_off, 16), CHUNK)
        y_out[rel] = (part[rel, other] + sib_in[rel, other].astype(F32)).astype(BF16)
        go(ry_copy(rel))
        own = pl.ds(pl.multiple_of(own_off, 16), CHUNK)
        part[rel, own] += sib_in[rel, own].astype(F32)
        part[rel, :SHARED] += sib_in[rel, :SHARED].astype(F32)

    def ring_copy(way, left_to_go, piece, off, rows):
        here = pl.ds(pl.multiple_of(off, 16), rows)
        return remote(
            ring_out.at[way, left_to_go - 1, here],
            ring_in.at[way, left_to_go - 1, here],
            r_send.at[way, left_to_go - 1, piece],
            r_recv.at[way, left_to_go - 1, piece],
            toward[way],
        )

    def rel_of(way, distance):
        return distance if way == RIGHT else (NZ - distance) % NZ

    def own_sum(rel, piece, off, rows):
        value = part[rel, pl.ds(pl.multiple_of(off, 16), rows)]
        if piece == OWN:
            value = value + y_in[rel].astype(F32)
        return value

    def emit(way, distance, piece, off, rows, value):
        here = pl.ds(pl.multiple_of(off, 16), rows)
        ring_out[way, distance - 1, here] = value.astype(BF16)
        go(ring_copy(way, distance, piece, off, rows))

    def incoming(way, distance, piece, off, rows):
        ring_copy(way, distance, piece, off, rows).wait_recv()
        return ring_in[way, distance - 1, pl.ds(pl.multiple_of(off, 16), rows)].astype(F32)

    gather_started = list(started)
    started.clear()
    prepare(4)
    prepare(3)
    join(4)
    for way, piece in ((RIGHT, C0), (LEFT, C0), (LEFT, C1)):
        spec = far[way, piece]
        emit(way, 4, piece, spec["off"], spec["rows"], own_sum(4, piece, **spec))
    prepare(5)
    join(3)
    ry_copy(4).wait_recv()
    spec = far[RIGHT, OWN]
    emit(RIGHT, 4, OWN, spec["off"], spec["rows"], own_sum(4, OWN, **spec))
    join(5)
    prepare(2)
    prepare(6)
    pieces = ((C0, 0), (C1, CHUNK), (OWN, own_off))
    for distance in (3, 2, 1):
        for piece, off in pieces:
            for way in (RIGHT, LEFT):
                rel = rel_of(way, distance)
                if piece == OWN:
                    ry_copy(rel).wait_recv()
                value = own_sum(rel, piece, off, CHUNK)
                if distance < 3:
                    value = value + incoming(way, distance + 1, piece, off, CHUNK)
                    emit(way, distance, piece, off, CHUNK, value)
                elif (way, piece) in far:
                    spec = far[way, piece]
                    arrived = incoming(way, 4, piece, spec["off"], spec["rows"])
                    if spec["rows"] == CHUNK:
                        value = value + arrived
                    elif way == RIGHT:
                        value = jnp.concatenate([value[:HALF] + arrived, value[HALF:]], axis=0)
                    else:
                        value = jnp.concatenate([value[:HALF], value[HALF:] + arrived], axis=0)
                    emit(way, distance, piece, off, CHUNK, value)
                else:
                    emit(way, distance, piece, off, CHUNK, value)
        if distance > 1:
            join(distance - 1)
            join(NZ - distance + 1)
            if distance == 3:
                prepare(1)
                prepare(7)
            else:
                prepare(0)
        else:
            join(0)
            for copy in gather_started:
                copy.wait_send()

    def send_back(q):
        sx, sy = seq_of(q)
        return remote(ret_out.at[q], ret.at[xy], b_send.at[q], b_recv.at[xy], plane(sx, sy))

    def is_me(q):
        sx, sy = seq_of(q)
        return (sx == x) & (sy == y)

    for piece, off in pieces:
        if piece == OWN:
            ry_copy(0).wait_recv()
        value = own_sum(0, piece, off, CHUNK)
        value = value + incoming(RIGHT, 1, piece, off, CHUNK)
        value = value + incoming(LEFT, 1, piece, off, CHUNK)
        first = {C0: 0, C1: 4, OWN: 8}[piece]
        value = jnp.concatenate(
            [value.reshape(4, CAP, COLS), jnp.zeros((4, PAD - CAP, COLS), F32)], axis=1
        )
        ret_out[first:first + 4] = value.astype(BF16)
        for q in range(first, first + 4):
            pl.when(jnp.logical_not(is_me(q)))(send_back(q).start)

    @pl.when(goes(y))
    def _():
        ret[xy] = ret_out[my_q]

    for i in range(16):
        @pl.when(jnp.logical_not(goes(i % 4)))
        def _():
            ret[i] = jnp.zeros((PAD, COLS), BF16)

    stat_copy(0, 2).wait_recv()
    totals = stat_src[2] + stat_c[...]
    domain_mean = totals[:, 0:1] / totals[:, 1:2]
    eye = lax.broadcasted_iota(jnp.int32, (EXPERTS, EXPERTS), 0) == lax.broadcasted_iota(
        jnp.int32, (EXPERTS, EXPERTS), 1
    )
    mean_row = jnp.sum(jnp.where(eye, domain_mean, 0.0), axis=0, keepdims=True)
    scaled = prior_ref[...] * jnp.exp(dro_step * mean_row)
    weights_ref[...] = EXPERTS * scaled / jnp.sum(scaled, axis=1, keepdims=True)

    for copy in started:
        copy.wait_send()
    for i in range(15):
        allowed_i, copy = send_block(i)
        pl.when(allowed_i)(copy.wait_send)
    for i in range(1, 4):
        stat_copy(i, 0).wait_send()
        stat_copy(i, 1).wait_send()
    stat_copy(0, 2).wait_send()

    place = lax.broadcasted_iota(jnp.int32, (TOK, 16 * PAD), 1).astype(F32)
    spot = label_col * (2 * PAD) + rank_col
    take = ((place == spot) | (place == spot + PAD)).astype(BF16)
    for i in range(16):
        arrival = remote(
            ret_out.at[0], ret.at[i], b_send.at[0], b_recv.at[i], plane(i // 4, i % 4)
        )
        pl.when(goes(i % 4) & (xy != i))(arrival.wait_recv)
    expert_out = jnp.dot(take, ret[...].reshape(16 * PAD, COLS), preferred_element_type=F32)
    mixed_ref[...] = (hidden[...].astype(F32) + expert_out).astype(BF16)
    for q in range(12):
        pl.when(jnp.logical_not(is_me(q)))(send_back(q).wait_send)


def body(
    residual, queries, key_rows, value_rows, lengths, labels, losses, prior_weights, norm_gain,
    gate_weight, up_weight, down_weight,
):
    vmem = pl.BlockSpec(memory_space=pltpu.VMEM)
    smem = pl.BlockSpec(memory_space=pltpu.SMEM)
    hbm = pl.BlockSpec(memory_space=pl.ANY)
    dma = pltpu.SemaphoreType.DMA
    tile = (TOK, COLS)
    mixed, weights = pl.pallas_call(
        kernel,
        out_shape=(
            jax.ShapeDtypeStruct(tile, BF16),
            jax.ShapeDtypeStruct((1, EXPERTS), F32),
        ),
        in_specs=[smem, vmem, vmem, vmem, vmem] + [hbm] * 7,
        out_specs=(vmem, vmem),
        scratch_shapes=[
            pltpu.VMEM(tile, BF16),
            pltpu.VMEM(tile, BF16),
            pltpu.VMEM(tile, BF16),
            pltpu.VMEM(tile, BF16),
            pltpu.VMEM((NZ * COLS, HID), BF16),
            pltpu.VMEM((NZ * COLS, HID), BF16),
            pltpu.VMEM((NZ, HID, COLS), BF16),
            pltpu.VMEM(tile, BF16),
            pltpu.VMEM((EXPERTS, PAD, COLS), BF16),
            pltpu.VMEM((12, PAD, COLS), BF16),
            pltpu.VMEM((NZ, ROWS, COLS), BF16),
            pltpu.VMEM((ROWS, HID), F32),
            pltpu.VMEM((ROWS, HID), F32),
            pltpu.VMEM((ROWS, 128), F32),
            pltpu.VMEM((ROWS, HID), BF16),
            pltpu.VMEM((NZ, CORE_ROWS, COLS), F32),
            pltpu.VMEM((NZ, CORE_ROWS, COLS), BF16),
            pltpu.VMEM((NZ, CORE_ROWS, COLS), BF16),
            pltpu.VMEM((2, 4, CORE_ROWS, COLS), BF16),
            pltpu.VMEM((2, 4, CORE_ROWS, COLS), BF16),
            pltpu.VMEM((NZ, CHUNK, COLS), BF16),
            pltpu.VMEM((NZ, CHUNK, COLS), BF16),
            pltpu.VMEM((12, PAD, COLS), BF16),
            pltpu.VMEM((16, PAD, COLS), BF16),
            pltpu.VMEM((4, EXPERTS, 128), F32),
            pltpu.VMEM((4, EXPERTS, 128), F32),
            pltpu.VMEM((EXPERTS, 128), F32),
            pltpu.VMEM((3, EXPERTS, 128), F32),
            dma((4,)), dma((2 + NZ,)),
            dma((15,)), dma((12,)),
            dma((2, 4, 3)), dma((2, 4, 3)),
            dma((NZ, 4)), dma((NZ, 4)),
            dma((NZ,)), dma((NZ,)),
            dma((NZ,)), dma((NZ,)),
            dma((NZ,)), dma((NZ,)),
            dma((2, 4, 3)), dma((2, 4, 3)),
            dma((12,)), dma((16,)),
            dma((7,)), dma((9,)),
        ],
        compiler_params=pltpu.CompilerParams(
            collective_id=0, has_side_effects=True, vmem_limit_bytes=60 * 1024 * 1024
        ),
    )(
        lengths, labels, losses.reshape(1, TOK), prior_weights.reshape(1, EXPERTS),
        norm_gain.reshape(NZ, COLS), residual, queries, key_rows, value_rows,
        gate_weight, up_weight, down_weight,
    )
    return (mixed, weights.reshape(EXPERTS))


def solution(mesh):
    placed = (
        P("dp", "mp"),
        P("dp", "mp"),
        P("dp", "mp"),
        P("dp", "mp"),
        P("dp", None),
        P("dp", None),
        P("dp"),
        P(),
        P(),
        P(None, ("dp", "mp")),
        P(None, ("dp", "mp")),
        P(("dp", "mp"), None),
    )
    return jax.shard_map(
        body, mesh=mesh, in_specs=placed, out_specs=(P("dp", "mp"), P()), check_vma=False
    )
```

```python
import jax
import jax.numpy as jnp
from jax import lax
from jax.experimental import pallas as pl
from jax.experimental.pallas import tpu as pltpu
from jax.sharding import PartitionSpec as P

HEAD_DIM = 128
EXPERTS = 8
CAP = 24
PAD = 32
TOK = 128
COLS = 512
HID = 344
NZ = 8
CORE_ROWS = 16 * CAP
ROWS = 2 * CORE_ROWS
CHUNK = 4 * CAP
SHARED = 2 * CHUNK
RIGHT, LEFT = 0, 1
F32, BF16 = jnp.float32, jnp.bfloat16
MESH = pl.DeviceIdType.MESH
NT = (((1,), (1,)), ((), ()))

dro_step = 0.5


def kernel(
    lengths_ref, labels_ref, losses_ref, prior_ref, gain_ref,
    res_hbm, q_hbm, k_hbm, v_hbm, gate_hbm, up_hbm, down_hbm,
    mixed_ref, weights_ref,
    res_v, q_v, k_v, v_v, gate_v, up_v, down_v,
    hidden, packed, stage, xb, acc_g, acc_u, square, inner,
    part, sib_out, sib_in, ring_in, ring_out, y_out, y_in, ret_out, ret,
    stat_x, stat_y, stat_c, stat_src,
    in_sem, w_sem, a_send, a_recv, g_send, g_recv, gs_send, gs_recv, gy_send, gy_recv,
    rs_send, rs_recv, ry_send, ry_recv, r_send, r_recv, b_send, b_recv, st_send, st_recv,
):
    dp = lax.axis_index("dp")
    z = lax.axis_index("mp")
    core = lax.rem(dp, 2)
    xy = dp // 2
    x, y = xy // 4, lax.rem(xy, 4)
    yb = lax.rem(y, 2)

    def plane(tx, ty, tc=None):
        return ((tx * 4 + ty) * 2 + (core if tc is None else tc), z)

    sibling = (dp + 1 - 2 * core, z)
    partner = plane(x, y + 1 - 2 * yb)
    z_right = (dp, lax.rem(z + 1, NZ))
    z_left = (dp, lax.rem(z + NZ - 1, NZ))
    toward = (z_right, z_left)
    offsets = [((i // 4), i % 4) for i in range(1, 16)]

    barrier = pltpu.get_barrier_semaphore()
    peers = [plane(lax.rem(x + dx, 4), lax.rem(y + dy, 4)) for dx, dy in offsets]
    peers += [sibling, z_right, z_left]
    for peer in peers:
        pl.semaphore_signal(barrier, inc=1, device_id=peer, device_id_type=MESH)

    loads = [
        pltpu.make_async_copy(src, dst, in_sem.at[i])
        for i, (src, dst) in enumerate(((q_hbm, q_v), (k_hbm, k_v), (v_hbm, v_v), (res_hbm, res_v)))
    ]
    for load in loads:
        load.start()
    weight_loads = [
        pltpu.make_async_copy(gate_hbm, gate_v, w_sem.at[0]),
        pltpu.make_async_copy(up_hbm, up_v, w_sem.at[1]),
    ] + [
        pltpu.make_async_copy(down_hbm.at[:, pl.ds(i * COLS, COLS)], down_v.at[i], w_sem.at[2 + i])
        for i in range(NZ)
    ]
    for load in weight_loads:
        load.start()

    def remote(src, dst, send, recv, device):
        return pltpu.make_async_remote_copy(
            src_ref=src, dst_ref=dst, send_sem=send, recv_sem=recv,
            device_id=device, device_id_type=MESH,
        )

    at0 = lax.broadcasted_iota(jnp.int32, (TOK, TOK), 0)
    at1 = lax.broadcasted_iota(jnp.int32, (TOK, TOK), 1)
    label_row = labels_ref[...].astype(F32)
    label_col = jnp.sum(jnp.where(at0 == at1, label_row, 0.0), axis=1, keepdims=True)
    same = label_col == label_row
    rank_row = jnp.sum(jnp.where(same & (at0 < at1), 1.0, 0.0), axis=0, keepdims=True)
    rank_col = jnp.sum(jnp.where(same & (at1 < at0), 1.0, 0.0), axis=1, keepdims=True)
    slot_row = label_row * PAD + rank_row
    slot_ids = lax.broadcasted_iota(jnp.int32, (EXPERTS * PAD, TOK), 0).astype(F32)
    select = (slot_ids == slot_row).astype(BF16)

    domain = lax.broadcasted_iota(jnp.int32, (EXPERTS, TOK), 0).astype(F32)
    lane = lax.broadcasted_iota(jnp.int32, (EXPERTS, TOK), 1)
    member = (domain == label_row).astype(F32)
    loss_sum = jnp.sum(member * losses_ref[...], axis=1, keepdims=True)
    count = jnp.sum(member, axis=1, keepdims=True)
    stat_src[0] = jnp.where(lane == 0, loss_sum, jnp.where(lane == 1, count, 0.0))

    ends = [lengths_ref[0, 0]]
    for i in range(1, 4):
        ends.append(ends[-1] + lengths_ref[0, i])
    doc0 = sum((at0 >= end).astype(jnp.int32) for end in ends)
    doc1 = sum((at1 >= end).astype(jnp.int32) for end in ends)
    allowed = (doc0 == doc1) & (at1 <= at0)
    for load in loads:
        load.wait()
    for head in range(COLS // HEAD_DIM):
        cut = slice(head * HEAD_DIM, (head + 1) * HEAD_DIM)
        scores = lax.dot_general(
            q_v[:, cut], k_v[:, cut], NT, preferred_element_type=F32
        ) * HEAD_DIM ** (-0.5)
        scores = jnp.where(allowed, scores, -1e30)
        exp_scores = jnp.exp(scores - jnp.max(scores, axis=1, keepdims=True))
        probs = (exp_scores / jnp.sum(exp_scores, axis=1, keepdims=True)).astype(BF16)
        attn = jnp.dot(probs, v_v[:, cut], preferred_element_type=F32)
        hidden[:, cut] = (res_v[:, cut].astype(F32) + attn).astype(BF16)
    packed[...] = (
        jnp.dot(select, hidden[...], preferred_element_type=F32)
        .astype(BF16)
        .reshape(EXPERTS, PAD, COLS)
    )

    pl.semaphore_wait(barrier, len(peers))

    my_q = jnp.where(x >= 2, (x - 2) * 4 + y, 8 + y)

    def goes(ty):
        return (x >= 2) | (lax.rem(ty, 2) == x)

    def send_block(i):
        dx, dy = offsets[i]
        tx, ty = lax.rem(x + dx, 4), lax.rem(y + dy, 4)
        copy = remote(
            packed.at[2 * tx + ty // 2], stage.at[my_q], a_send.at[i], a_recv.at[my_q], plane(tx, ty)
        )
        return goes(ty), copy

    for i in range(15):
        allowed_i, copy = send_block(i)
        pl.when(allowed_i)(copy.start)

    @pl.when(goes(y))
    def _():
        stage[my_q] = packed[2 * x + y // 2]

    def seq_of(q):
        if q < 8:
            return 2 + q // 4, q % 4
        return yb, q - 8

    def stat_copy(i, phase):
        if phase == 0:
            dst, peer = stat_x, plane(lax.rem(x + i, 4), y)
            return remote(stat_src.at[0], dst.at[x], st_send.at[i - 1], st_recv.at[x], peer)
        if phase == 1:
            dst, peer = stat_y, plane(x, lax.rem(y + i, 4))
            return remote(stat_src.at[1], dst.at[y], st_send.at[2 + i], st_recv.at[4 + y], peer)
        return remote(stat_src.at[2], stat_c, st_send.at[6], st_recv.at[8], sibling)

    def stat_wait(i, phase):
        if phase == 0:
            at = lax.rem(x + i, 4)
            return remote(stat_src.at[0], stat_x.at[at], st_send.at[0], st_recv.at[at], plane(at, y))
        at = lax.rem(y + i, 4)
        return remote(stat_src.at[1], stat_y.at[at], st_send.at[0], st_recv.at[4 + at], plane(x, at))

    for i in range(1, 4):
        stat_copy(i, 0).start()
    stat_x[x] = stat_src[0]

    base = core * CORE_ROWS
    sib_base = (1 - core) * CORE_ROWS
    own_off = SHARED + yb * CHUNK
    other_off = SHARED + (1 - yb) * CHUNK
    OWN, C0, C1, OTHER = 0, 1, 2, 3
    piece_off = (own_off, 0, CHUNK, other_off)

    def slice_at(rel):
        return lax.rem(z + rel, NZ)

    def block(rel, off, rows):
        start = pl.multiple_of(base + off, 16)
        return xb.at[slice_at(rel), pl.ds(start, rows)]

    def gather_copy(way, hop, piece, sending, off=None, rows=CHUNK):
        sign = 1 if way == LEFT else -1
        behind = hop - 1 if sending else hop
        rel = (sign * behind) % NZ
        ref = block(rel, piece_off[piece] if off is None else off, rows)
        return remote(
            ref, ref, g_send.at[way, hop - 1, piece], g_recv.at[way, hop - 1, piece], toward[way]
        )

    HALF = CHUNK // 2
    far = {
        (RIGHT, OWN): dict(off=own_off, rows=CHUNK),
        (RIGHT, C0): dict(off=0, rows=HALF),
        (LEFT, C0): dict(off=HALF, rows=HALF),
        (LEFT, C1): dict(off=CHUNK, rows=CHUNK),
    }

    def sib_copy(rel, piece, mine=True):
        start = pl.multiple_of((base if mine else sib_base) + piece_off[piece], 16)
        ref = xb.at[slice_at(rel), pl.ds(start, CHUNK)]
        return remote(ref, ref, gs_send.at[rel, piece], gs_recv.at[rel, piece], sibling)

    def y_copy(rel, mine=True):
        ref = block(rel, own_off if mine else other_off, CHUNK)
        return remote(ref, ref, gy_send.at[rel], gy_recv.at[rel], partner)

    started = []

    def go(copy):
        copy.start()
        started.append(copy)

    def spread(rel, piece):
        if piece == OWN:
            go(y_copy(rel))
        go(sib_copy(rel, piece))

    for piece, first in ((OWN, 8), (C0, 0), (C1, 4)):
        for q in range(first, first + 4):
            sx, sy = seq_of(q)
            arrival = remote(
                packed.at[0], stage.at[q], a_send.at[0], a_recv.at[q], plane(sx, sy)
            )
            pl.when((sx != x) | (sy != y))(arrival.wait_recv)
        rows = stage[first:first + 4].astype(F32)[:, :CAP].reshape(CHUNK, COLS).astype(BF16)
        start = pl.multiple_of(base + piece_off[piece], 16)
        xb[z, pl.ds(start, CHUNK)] = rows
        go(gather_copy(RIGHT, 1, piece, True))
        go(gather_copy(LEFT, 1, piece, True))
        spread(0, piece)

    for ref in (acc_g, acc_u, square):
        ref[...] = jnp.zeros_like(ref)

    BLOCK = SHARED

    def multiply(rels, rows_from):
        def one(i, carry):
            rel = rels[0] if len(rels) == 1 else jnp.where(i == 0, rels[0], rels[1])
            s = slice_at(rel)
            at = pl.multiple_of(s * COLS, COLS)
            gain = gain_ref[:, pl.ds(at, COLS)]
            for start in rows_from:
                here = pl.ds(pl.multiple_of(start, 16), BLOCK)
                value = xb[s, here, :].astype(F32)
                sq = value * value
                square[here, :] += (
                    sq[:, :128] + sq[:, 128:256] + sq[:, 256:384] + sq[:, 384:]
                )
                scaled = (value * gain).astype(BF16)
                acc_g[here, :] += lax.dot_general(
                    scaled, gate_v[:, pl.ds(at, COLS)], NT, preferred_element_type=F32
                )
                acc_u[here, :] += lax.dot_general(
                    scaled, up_v[:, pl.ds(at, COLS)], NT, preferred_element_type=F32
                )
            return carry

        lax.fori_loop(0, len(rels), one, 0)

    def settle(rels, j):
        if j == 0:
            for rel in rels:
                y_copy(rel, mine=False).wait_recv()
                go(sib_copy(rel, OTHER))
            multiply(rels, (base,))
        elif j == 1:
            for rel in rels:
                sib_copy(rel, C0, mine=False).wait_recv()
                sib_copy(rel, C1, mine=False).wait_recv()
            multiply(rels, (sib_base,))
        else:
            for rel in rels:
                sib_copy(rel, OWN, mine=False).wait_recv()
                sib_copy(rel, OTHER, mine=False).wait_recv()
            multiply(rels, (base + SHARED, sib_base + SHARED))

    weight_loads[0].wait()
    weight_loads[1].wait()
    before = (0,)
    for hop in (1, 2, 3):
        for j, piece in enumerate((OWN, C0, C1)):
            for way in (RIGHT, LEFT):
                gather_copy(way, hop, piece, False).wait_recv()
                if hop < 3:
                    go(gather_copy(way, hop + 1, piece, True))
                elif (way, piece) in far:
                    go(gather_copy(way, 4, piece, True, **far[way, piece]))
                spread(hop if way == LEFT else NZ - hop, piece)
            settle(before, j)
        before = (hop, NZ - hop)
        if hop == 1:
            for i in range(1, 4):
                stat_wait(i, 0).wait_recv()
            stat_src[1] = (stat_x[0] + stat_x[1]) + (stat_x[2] + stat_x[3])
            for i in range(1, 4):
                stat_copy(i, 1).start()
            stat_y[y] = stat_src[1]
        if hop == 2:
            for i in range(1, 4):
                stat_wait(i, 1).wait_recv()
            stat_src[2] = (stat_y[0] + stat_y[1]) + (stat_y[2] + stat_y[3])
            stat_copy(0, 2).start()
    gather_copy(RIGHT, 4, OWN, False, **far[RIGHT, OWN]).wait_recv()
    spread(4, OWN)
    settle(before, 0)
    gather_copy(RIGHT, 4, C0, False, **far[RIGHT, C0]).wait_recv()
    gather_copy(LEFT, 4, C0, False, **far[LEFT, C0]).wait_recv()
    spread(4, C0)
    settle(before, 1)
    gather_copy(LEFT, 4, C1, False, **far[LEFT, C1]).wait_recv()
    spread(4, C1)
    settle(before, 2)
    for j in range(3):
        settle((4,), j)

    def activate(i, carry):
        here = pl.ds(pl.multiple_of(i * BLOCK, BLOCK), BLOCK)
        mean = jnp.sum(square[here, :], axis=1, keepdims=True) * (1.0 / (NZ * COLS))
        scale = lax.rsqrt(mean + 1e-05)
        gate = acc_g[here, :] * scale
        up = acc_u[here, :] * scale
        inner[here, :] = (gate / (1.0 + jnp.exp(-gate)) * up).astype(BF16)
        return carry

    lax.fori_loop(0, ROWS // BLOCK, activate, 0)
    for load in weight_loads[2:]:
        load.wait()

    def rs_copy(rel):
        return remote(
            sib_out.at[rel], sib_in.at[rel], rs_send.at[rel], rs_recv.at[rel], sibling
        )

    def ry_copy(rel):
        return remote(y_out.at[rel], y_in.at[rel], ry_send.at[rel], ry_recv.at[rel], partner)

    def prepare(rel):
        weight = down_v.at[slice_at(rel)]

        def one(i, carry):
            off = pl.multiple_of(i * BLOCK, BLOCK)
            theirs = inner[pl.ds(pl.multiple_of(sib_base + off, 16), BLOCK), :]
            sib_out[rel, pl.ds(off, BLOCK)] = jnp.dot(
                theirs, weight[...], preferred_element_type=F32
            ).astype(BF16)
            return carry

        lax.fori_loop(0, 2, one, 0)
        go(rs_copy(rel))

        def two(i, carry):
            off = pl.multiple_of(i * BLOCK, BLOCK)
            mine = inner[pl.ds(pl.multiple_of(base + off, 16), BLOCK), :]
            part[rel, pl.ds(off, BLOCK)] = jnp.dot(mine, weight[...], preferred_element_type=F32)
            return carry

        lax.fori_loop(0, 2, two, 0)

    def join(rel):
        rs_copy(rel).wait_recv()
        other = pl.ds(pl.multiple_of(other_off, 16), CHUNK)
        y_out[rel] = (part[rel, other] + sib_in[rel, other].astype(F32)).astype(BF16)
        go(ry_copy(rel))
        own = pl.ds(pl.multiple_of(own_off, 16), CHUNK)
        part[rel, own] += sib_in[rel, own].astype(F32)
        part[rel, :SHARED] += sib_in[rel, :SHARED].astype(F32)

    def ring_copy(way, left_to_go, piece, off, rows):
        here = pl.ds(pl.multiple_of(off, 16), rows)
        return remote(
            ring_out.at[way, left_to_go - 1, here],
            ring_in.at[way, left_to_go - 1, here],
            r_send.at[way, left_to_go - 1, piece],
            r_recv.at[way, left_to_go - 1, piece],
            toward[way],
        )

    def rel_of(way, distance):
        return distance if way == RIGHT else (NZ - distance) % NZ

    def own_sum(rel, piece, off, rows):
        value = part[rel, pl.ds(pl.multiple_of(off, 16), rows)]
        if piece == OWN:
            value = value + y_in[rel].astype(F32)
        return value

    def emit(way, distance, piece, off, rows, value):
        here = pl.ds(pl.multiple_of(off, 16), rows)
        ring_out[way, distance - 1, here] = value.astype(BF16)
        go(ring_copy(way, distance, piece, off, rows))

    def incoming(way, distance, piece, off, rows):
        ring_copy(way, distance, piece, off, rows).wait_recv()
        return ring_in[way, distance - 1, pl.ds(pl.multiple_of(off, 16), rows)].astype(F32)

    gather_started = list(started)
    started.clear()
    prepare(4)
    prepare(3)
    join(4)
    for way, piece in ((RIGHT, C0), (LEFT, C0), (LEFT, C1)):
        spec = far[way, piece]
        emit(way, 4, piece, spec["off"], spec["rows"], own_sum(4, piece, **spec))
    prepare(5)
    join(3)
    ry_copy(4).wait_recv()
    spec = far[RIGHT, OWN]
    emit(RIGHT, 4, OWN, spec["off"], spec["rows"], own_sum(4, OWN, **spec))
    join(5)
    prepare(2)
    prepare(6)
    pieces = ((C0, 0), (C1, CHUNK), (OWN, own_off))
    for distance in (3, 2, 1):
        for piece, off in pieces:
            for way in (RIGHT, LEFT):
                rel = rel_of(way, distance)
                if piece == OWN:
                    ry_copy(rel).wait_recv()
                value = own_sum(rel, piece, off, CHUNK)
                if distance < 3:
                    value = value + incoming(way, distance + 1, piece, off, CHUNK)
                    emit(way, distance, piece, off, CHUNK, value)
                elif (way, piece) in far:
                    spec = far[way, piece]
                    arrived = incoming(way, 4, piece, spec["off"], spec["rows"])
                    if spec["rows"] == CHUNK:
                        value = value + arrived
                    elif way == RIGHT:
                        value = jnp.concatenate([value[:HALF] + arrived, value[HALF:]], axis=0)
                    else:
                        value = jnp.concatenate([value[:HALF], value[HALF:] + arrived], axis=0)
                    emit(way, distance, piece, off, CHUNK, value)
                else:
                    emit(way, distance, piece, off, CHUNK, value)
        if distance > 1:
            join(distance - 1)
            join(NZ - distance + 1)
            if distance == 3:
                prepare(1)
                prepare(7)
            else:
                prepare(0)
        else:
            join(0)
            for copy in gather_started:
                copy.wait_send()

    def send_back(q):
        sx, sy = seq_of(q)
        return remote(ret_out.at[q], ret.at[xy], b_send.at[q], b_recv.at[xy], plane(sx, sy))

    def is_me(q):
        sx, sy = seq_of(q)
        return (sx == x) & (sy == y)

    for piece, off in pieces:
        if piece == OWN:
            ry_copy(0).wait_recv()
        value = own_sum(0, piece, off, CHUNK)
        value = value + incoming(RIGHT, 1, piece, off, CHUNK)
        value = value + incoming(LEFT, 1, piece, off, CHUNK)
        first = {C0: 0, C1: 4, OWN: 8}[piece]
        value = jnp.concatenate(
            [value.reshape(4, CAP, COLS), jnp.zeros((4, PAD - CAP, COLS), F32)], axis=1
        )
        ret_out[first:first + 4] = value.astype(BF16)
        for q in range(first, first + 4):
            pl.when(jnp.logical_not(is_me(q)))(send_back(q).start)

    @pl.when(goes(y))
    def _():
        ret[xy] = ret_out[my_q]

    for i in range(16):
        @pl.when(jnp.logical_not(goes(i % 4)))
        def _():
            ret[i] = jnp.zeros((PAD, COLS), BF16)

    stat_copy(0, 2).wait_recv()
    totals = stat_src[2] + stat_c[...]
    domain_mean = totals[:, 0:1] / totals[:, 1:2]
    eye = lax.broadcasted_iota(jnp.int32, (EXPERTS, EXPERTS), 0) == lax.broadcasted_iota(
        jnp.int32, (EXPERTS, EXPERTS), 1
    )
    mean_row = jnp.sum(jnp.where(eye, domain_mean, 0.0), axis=0, keepdims=True)
    scaled = prior_ref[...] * jnp.exp(dro_step * mean_row)
    weights_ref[...] = EXPERTS * scaled / jnp.sum(scaled, axis=1, keepdims=True)

    for copy in started:
        copy.wait_send()
    for i in range(15):
        allowed_i, copy = send_block(i)
        pl.when(allowed_i)(copy.wait_send)
    for i in range(1, 4):
        stat_copy(i, 0).wait_send()
        stat_copy(i, 1).wait_send()
    stat_copy(0, 2).wait_send()

    place = lax.broadcasted_iota(jnp.int32, (TOK, 16 * PAD), 1).astype(F32)
    spot = label_col * (2 * PAD) + rank_col
    take = ((place == spot) | (place == spot + PAD)).astype(BF16)
    for i in range(16):
        arrival = remote(
            ret_out.at[0], ret.at[i], b_send.at[0], b_recv.at[i], plane(i // 4, i % 4)
        )
        pl.when(goes(i % 4) & (xy != i))(arrival.wait_recv)
    expert_out = jnp.dot(take, ret[...].reshape(16 * PAD, COLS), preferred_element_type=F32)
    mixed_ref[...] = (hidden[...].astype(F32) + expert_out).astype(BF16)
    for q in range(12):
        pl.when(jnp.logical_not(is_me(q)))(send_back(q).wait_send)


def body(
    residual, queries, key_rows, value_rows, lengths, labels, losses, prior_weights, norm_gain,
    gate_weight, up_weight, down_weight,
):
    vmem = pl.BlockSpec(memory_space=pltpu.VMEM)
    smem = pl.BlockSpec(memory_space=pltpu.SMEM)
    hbm = pl.BlockSpec(memory_space=pl.ANY)
    dma = pltpu.SemaphoreType.DMA
    tile = (TOK, COLS)
    mixed, weights = pl.pallas_call(
        kernel,
        out_shape=(
            jax.ShapeDtypeStruct(tile, BF16),
            jax.ShapeDtypeStruct((1, EXPERTS), F32),
        ),
        in_specs=[smem, vmem, vmem, vmem, vmem] + [hbm] * 7,
        out_specs=(vmem, vmem),
        scratch_shapes=[
            pltpu.VMEM(tile, BF16),
            pltpu.VMEM(tile, BF16),
            pltpu.VMEM(tile, BF16),
            pltpu.VMEM(tile, BF16),
            pltpu.VMEM((HID, NZ * COLS), BF16),
            pltpu.VMEM((HID, NZ * COLS), BF16),
            pltpu.VMEM((NZ, HID, COLS), BF16),
            pltpu.VMEM(tile, BF16),
            pltpu.VMEM((EXPERTS, PAD, COLS), BF16),
            pltpu.VMEM((12, PAD, COLS), BF16),
            pltpu.VMEM((NZ, ROWS, COLS), BF16),
            pltpu.VMEM((ROWS, HID), F32),
            pltpu.VMEM((ROWS, HID), F32),
            pltpu.VMEM((ROWS, 128), F32),
            pltpu.VMEM((ROWS, HID), BF16),
            pltpu.VMEM((NZ, CORE_ROWS, COLS), F32),
            pltpu.VMEM((NZ, CORE_ROWS, COLS), BF16),
            pltpu.VMEM((NZ, CORE_ROWS, COLS), BF16),
            pltpu.VMEM((2, 4, CORE_ROWS, COLS), BF16),
            pltpu.VMEM((2, 4, CORE_ROWS, COLS), BF16),
            pltpu.VMEM((NZ, CHUNK, COLS), BF16),
            pltpu.VMEM((NZ, CHUNK, COLS), BF16),
            pltpu.VMEM((12, PAD, COLS), BF16),
            pltpu.VMEM((16, PAD, COLS), BF16),
            pltpu.VMEM((4, EXPERTS, 128), F32),
            pltpu.VMEM((4, EXPERTS, 128), F32),
            pltpu.VMEM((EXPERTS, 128), F32),
            pltpu.VMEM((3, EXPERTS, 128), F32),
            dma((4,)), dma((2 + NZ,)),
            dma((15,)), dma((12,)),
            dma((2, 4, 3)), dma((2, 4, 3)),
            dma((NZ, 4)), dma((NZ, 4)),
            dma((NZ,)), dma((NZ,)),
            dma((NZ,)), dma((NZ,)),
            dma((NZ,)), dma((NZ,)),
            dma((2, 4, 3)), dma((2, 4, 3)),
            dma((12,)), dma((16,)),
            dma((7,)), dma((9,)),
        ],
        compiler_params=pltpu.CompilerParams(
            collective_id=0, has_side_effects=True, vmem_limit_bytes=60 * 1024 * 1024
        ),
    )(
        lengths, labels.reshape(1, TOK), losses.reshape(1, TOK), prior_weights.reshape(1, EXPERTS),
        norm_gain.reshape(1, NZ * COLS), residual, queries, key_rows, value_rows,
        gate_weight.T, up_weight.T, down_weight,
    )
    return (mixed, weights.reshape(EXPERTS))


def solution(mesh):
    placed = (
        P("dp", "mp"),
        P("dp", "mp"),
        P("dp", "mp"),
        P("dp", "mp"),
        P("dp", None),
        P("dp", None),
        P("dp"),
        P(),
        P(),
        P(None, ("dp", "mp")),
        P(None, ("dp", "mp")),
        P(("dp", "mp"), None),
    )
    return jax.shard_map(
        body, mesh=mesh, in_specs=placed, out_specs=(P("dp", "mp"), P()), check_vma=False
    )
```

```python
import jax
import jax.numpy as jnp
from jax import lax
from jax.experimental import pallas as pl
from jax.experimental.pallas import tpu as pltpu
from jax.sharding import PartitionSpec as P

HEAD_DIM = 128
EXPERTS = 8
CAP = 24
TOK = 128
COLS = 512
HID = 344
HALF_N = 384
NZ = 8
CORE_ROWS = 16 * CAP
ROWS = 2 * CORE_ROWS
CHUNK = 4 * CAP
HALF = CHUNK // 2
WIDE = COLS // 2
SHARED = 2 * CHUNK
RIGHT, LEFT = 0, 1
F32, BF16 = jnp.float32, jnp.bfloat16
MESH = pl.DeviceIdType.MESH
NT = (((1,), (1,)), ((), ()))

dro_step = 0.5


def kernel(
    lengths_ref, labels_ref, losses_ref, prior_ref, gain_ref,
    res_hbm, q_hbm, k_hbm, v_hbm, gate_hbm, up_hbm, down_hbm,
    mixed_ref, weights_ref,
    res_v, q_v, k_v, v_v, gate_v, up_v, down_v, both_v,
    hidden, packed, stage, xb, acc, square, inner,
    part, sib_out, sib_in, ring_in, ring_out, y_out, y_in, ret_out, ret,
    stat_x, stat_y, stat_c, stat_src,
    in_sem, w_sem, a_send, a_recv, g_send, g_recv, gs_send, gs_recv, gy_send, gy_recv,
    rs_send, rs_recv, ry_send, ry_recv, r_send, r_recv, b_send, b_recv, st_send, st_recv,
):
    dp = lax.axis_index("dp")
    z = lax.axis_index("mp")
    core = lax.rem(dp, 2)
    xy = dp // 2
    x, y = xy // 4, lax.rem(xy, 4)
    yb = lax.rem(y, 2)

    def plane(tx, ty, tc=None):
        return ((tx * 4 + ty) * 2 + (core if tc is None else tc), z)

    sibling = (dp + 1 - 2 * core, z)
    partner = plane(x, y + 1 - 2 * yb)
    z_right = (dp, lax.rem(z + 1, NZ))
    z_left = (dp, lax.rem(z + NZ - 1, NZ))
    toward = (z_right, z_left)
    offsets = [((i // 4), i % 4) for i in range(1, 16)]

    barrier = pltpu.get_barrier_semaphore()
    peers = [plane(lax.rem(x + dx, 4), lax.rem(y + dy, 4)) for dx, dy in offsets]
    peers += [sibling, z_right, z_left]
    for peer in peers:
        pl.semaphore_signal(barrier, inc=1, device_id=peer, device_id_type=MESH)

    loads = [
        pltpu.make_async_copy(src, dst, in_sem.at[i])
        for i, (src, dst) in enumerate(((q_hbm, q_v), (k_hbm, k_v), (v_hbm, v_v), (res_hbm, res_v)))
    ]
    for load in loads:
        load.start()
    weight_loads = [
        pltpu.make_async_copy(gate_hbm, gate_v, w_sem.at[0]),
        pltpu.make_async_copy(up_hbm, up_v, w_sem.at[1]),
    ] + [
        pltpu.make_async_copy(down_hbm.at[:, pl.ds(i * COLS, COLS)], down_v.at[i], w_sem.at[2 + i])
        for i in range(NZ)
    ]
    for load in weight_loads:
        load.start()

    def remote(src, dst, send, recv, device):
        return pltpu.make_async_remote_copy(
            src_ref=src, dst_ref=dst, send_sem=send, recv_sem=recv,
            device_id=device, device_id_type=MESH,
        )

    at0 = lax.broadcasted_iota(jnp.int32, (TOK, TOK), 0)
    at1 = lax.broadcasted_iota(jnp.int32, (TOK, TOK), 1)
    label_row = labels_ref[...].astype(F32)
    label_col = jnp.sum(jnp.where(at0 == at1, label_row, 0.0), axis=1, keepdims=True)
    same = label_col == label_row
    rank_row = jnp.sum(jnp.where(same & (at0 < at1), 1.0, 0.0), axis=0, keepdims=True)
    rank_col = jnp.sum(jnp.where(same & (at1 < at0), 1.0, 0.0), axis=1, keepdims=True)
    slot_row = label_row * (2 * CAP) + rank_row
    slot_ids = lax.broadcasted_iota(jnp.int32, (EXPERTS * 2 * CAP, TOK), 0).astype(F32)
    select = [(slot_ids == slot_row + half * CAP).astype(BF16) for half in range(2)]

    domain = lax.broadcasted_iota(jnp.int32, (EXPERTS, TOK), 0).astype(F32)
    lane = lax.broadcasted_iota(jnp.int32, (EXPERTS, TOK), 1)
    member = (domain == label_row).astype(F32)
    loss_sum = jnp.sum(member * losses_ref[...], axis=1, keepdims=True)
    count = jnp.sum(member, axis=1, keepdims=True)
    stat_src[0] = jnp.where(lane == 0, loss_sum, jnp.where(lane == 1, count, 0.0))

    ends = [lengths_ref[0, 0]]
    for i in range(1, 4):
        ends.append(ends[-1] + lengths_ref[0, i])
    doc0 = sum((at0 >= end).astype(jnp.int32) for end in ends)
    doc1 = sum((at1 >= end).astype(jnp.int32) for end in ends)
    allowed = (doc0 == doc1) & (at1 <= at0)
    for load in loads:
        load.wait()
    for head in range(COLS // HEAD_DIM):
        cut = slice(head * HEAD_DIM, (head + 1) * HEAD_DIM)
        scores = lax.dot_general(
            q_v[:, cut], k_v[:, cut], NT, preferred_element_type=F32
        ) * HEAD_DIM ** (-0.5)
        scores = jnp.where(allowed, scores, -1e30)
        exp_scores = jnp.exp(scores - jnp.max(scores, axis=1, keepdims=True))
        probs = (exp_scores / jnp.sum(exp_scores, axis=1, keepdims=True)).astype(BF16)
        attn = jnp.dot(probs, v_v[:, cut], preferred_element_type=F32)
        hidden[:, cut] = (res_v[:, cut].astype(F32) + attn).astype(BF16)
    packed[...] = (
        (
            jnp.dot(select[0], hidden[:, :WIDE], preferred_element_type=F32)
            + jnp.dot(select[1], hidden[:, WIDE:], preferred_element_type=F32)
        )
        .astype(BF16)
        .reshape(EXPERTS, 2 * CAP, WIDE)
    )

    pl.semaphore_wait(barrier, len(peers))

    my_q = jnp.where(x >= 2, (x - 2) * 4 + y, 8 + y)

    def goes(ty):
        return (x >= 2) | (lax.rem(ty, 2) == x)

    def send_block(i):
        dx, dy = offsets[i]
        tx, ty = lax.rem(x + dx, 4), lax.rem(y + dy, 4)
        copy = remote(
            packed.at[2 * tx + ty // 2], stage.at[my_q], a_send.at[i], a_recv.at[my_q], plane(tx, ty)
        )
        return goes(ty), copy

    for i in range(15):
        allowed_i, copy = send_block(i)
        pl.when(allowed_i)(copy.start)

    @pl.when(goes(y))
    def _():
        stage[my_q] = packed[2 * x + y // 2]

    def seq_of(q):
        if q < 8:
            return 2 + q // 4, q % 4
        return yb, q - 8

    def stat_copy(i, phase):
        if phase == 0:
            dst, peer = stat_x, plane(lax.rem(x + i, 4), y)
            return remote(stat_src.at[0], dst.at[x], st_send.at[i - 1], st_recv.at[x], peer)
        if phase == 1:
            dst, peer = stat_y, plane(x, lax.rem(y + i, 4))
            return remote(stat_src.at[1], dst.at[y], st_send.at[2 + i], st_recv.at[4 + y], peer)
        return remote(stat_src.at[2], stat_c, st_send.at[6], st_recv.at[8], sibling)

    def stat_wait(i, phase):
        if phase == 0:
            at = lax.rem(x + i, 4)
            return remote(stat_src.at[0], stat_x.at[at], st_send.at[0], st_recv.at[at], plane(at, y))
        at = lax.rem(y + i, 4)
        return remote(stat_src.at[1], stat_y.at[at], st_send.at[0], st_recv.at[4 + at], plane(x, at))

    def stats(step):
        if step == 0:
            for i in range(1, 4):
                stat_copy(i, 0).start()
            stat_x[x] = stat_src[0]
        elif step == 1:
            for i in range(1, 4):
                stat_wait(i, 0).wait_recv()
            stat_src[1] = (stat_x[0] + stat_x[1]) + (stat_x[2] + stat_x[3])
            for i in range(1, 4):
                stat_copy(i, 1).start()
            stat_y[y] = stat_src[1]
        elif step == 2:
            for i in range(1, 4):
                stat_wait(i, 1).wait_recv()
            stat_src[2] = (stat_y[0] + stat_y[1]) + (stat_y[2] + stat_y[3])
            stat_copy(0, 2).start()
        else:
            stat_copy(0, 2).wait_recv()
            totals = stat_src[2] + stat_c[...]
            domain_mean = totals[:, 0:1] / totals[:, 1:2]
            eye = lax.broadcasted_iota(jnp.int32, (EXPERTS, EXPERTS), 0) == lax.broadcasted_iota(
                jnp.int32, (EXPERTS, EXPERTS), 1
            )
            mean_row = jnp.sum(jnp.where(eye, domain_mean, 0.0), axis=0, keepdims=True)
            scaled = prior_ref[...] * jnp.exp(dro_step * mean_row)
            weights_ref[...] = EXPERTS * scaled / jnp.sum(scaled, axis=1, keepdims=True)

    acc[...] = jnp.zeros_like(acc)
    square[...] = jnp.zeros_like(square)
    for i in range(16):
        @pl.when(jnp.logical_not(goes(i % 4)))
        def _():
            ret[i] = jnp.zeros((2 * CAP, WIDE), BF16)

    for load in weight_loads:
        load.wait()

    def turn(i, carry):
        at = pl.ds(pl.multiple_of(i * COLS, COLS), COLS)
        for half, source in enumerate((gate_v, up_v)):
            first = half * HALF_N
            both_v[at, first + HALF_N - 128:first + HALF_N] = jnp.zeros((COLS, 128), BF16)
            both_v[at, first:first + HID] = source[:, at].T
        return carry

    lax.fori_loop(0, NZ, turn, 0)

    own_off = SHARED + yb * CHUNK
    other_off = SHARED + (1 - yb) * CHUNK
    OWN, C0, C1, OTHER = 0, 1, 2, 3
    piece_off = (own_off, 0, CHUNK, other_off)
    b_first = 2 * SHARED
    own_at = (b_first + yb * CHUNK, 0, SHARED, b_first + (1 - yb) * CHUNK)
    sib_at = tuple(
        at + step for at, step in zip(own_at, (SHARED, CHUNK, CHUNK, SHARED), strict=True)
    )
    groups = {
        "a": (0, 2 * SHARED, 0, SHARED, (C0, C1)),
        "c0": (0, SHARED, 0, CHUNK, (C0,)),
        "c1": (SHARED, SHARED, CHUNK, CHUNK, (C1,)),
        "b": (b_first, 2 * SHARED, SHARED, SHARED, (OWN, OTHER)),
    }
    group_sem = {"a": 0, "c0": 0, "c1": 1, "b": 2}
    lanes = {"B": (OWN, OWN), "C0": (C0, C0), "C1": (C1, C1), "A0": (C0, C1), "A1": (C1, C0)}
    first_q = {C0: 0, C1: 4, OWN: 8}

    def slice_at(rel):
        return lax.rem(z + rel, NZ)

    def rel_of(way, distance):
        return distance if way == RIGHT else (NZ - distance) % NZ

    def rows_at(off, rows):
        if isinstance(off, int):
            return pl.ds(off, rows)
        return pl.ds(pl.multiple_of(off, 16), rows)

    def part_of(way, lane, distance):
        if distance < 4 or lane in ("A0", "A1"):
            return 0, CHUNK
        return way * HALF, HALF

    started = []

    def go(copy):
        copy.start()
        started.append(copy)

    def gather_copy(way, hop, lane, sending):
        rel = rel_of(1 - way, hop - 1 if sending else hop)
        piece = lanes[lane][way]
        first, rows = part_of(way, lane, hop)
        ref = xb.at[slice_at(rel), rows_at(own_at[piece] + first, rows)]
        at = (way, hop - 1, piece)
        return remote(ref, ref, g_send.at[at], g_recv.at[at], toward[way])

    def sib_copy(rel, piece):
        return remote(
            xb.at[slice_at(rel), rows_at(own_at[piece], CHUNK)],
            xb.at[slice_at(rel), rows_at(sib_at[piece], CHUNK)],
            gs_send.at[rel, piece], gs_recv.at[rel, piece], sibling,
        )

    def y_copy(rel, mine=True):
        ref = xb.at[slice_at(rel), rows_at(own_at[OWN if mine else OTHER], CHUNK)]
        return remote(ref, ref, gy_send.at[rel], gy_recv.at[rel], partner)

    def spread(rel, piece):
        if piece == OWN:
            go(y_copy(rel))
        go(sib_copy(rel, piece))

    def start(piece):
        first = first_q[piece]
        for q in range(first, first + 4):
            sx, sy = seq_of(q)
            arrival = remote(
                packed.at[0], stage.at[q], a_send.at[0], a_recv.at[q], plane(sx, sy)
            )
            pl.when((sx != x) | (sy != y))(arrival.wait_recv)
        blocks = stage[first:first + 4].astype(F32)
        here = rows_at(own_at[piece], CHUNK)
        for half in range(2):
            xb[z, here, half * WIDE:(half + 1) * WIDE] = (
                blocks[:, half * CAP:(half + 1) * CAP].reshape(CHUNK, WIDE).astype(BF16)
            )

    def first_hop(lane):
        for way in (RIGHT, LEFT):
            go(gather_copy(way, 1, lane, True))

    def own_spread(piece):
        spread(0, piece)

    def hop(lane, h):
        for way in (RIGHT, LEFT):
            gather_copy(way, h, lane, False).wait_recv()
            if h < 3 or (h == 3 and lane != "A1"):
                go(gather_copy(way, h + 1, lane, True))
        first, second = lanes[lane]
        if h == 4 and first == second:
            spread(4, first)
            return
        for way in (RIGHT, LEFT):
            spread(rel_of(1 - way, h), lanes[lane][way])

    def y_arrive(*rels):
        for rel in rels:
            y_copy(rel, mine=False).wait_recv()
            go(sib_copy(rel, OTHER))

    def multiply(group, *rels):
        first, rows, _, _, pieces = groups[group]
        here = pl.ds(first, rows)
        for rel in rels:
            for piece in pieces:
                sib_copy(rel, piece).wait_recv()
            s = slice_at(rel)
            at = pl.ds(pl.multiple_of(s * COLS, COLS), COLS)
            value = xb[s, here, :].astype(F32)
            sq = value * value
            square[here, :] += sq[:, :128] + sq[:, 128:256] + sq[:, 256:384] + sq[:, 384:]
            scaled = (value * gain_ref[:, at]).astype(BF16)
            acc[here, :] += jnp.dot(scaled, both_v[at, :], preferred_element_type=F32)

    def activate(group):
        first, rows = groups[group][:2]
        here = pl.ds(first, rows)
        mean = jnp.sum(square[here, :], axis=1, keepdims=True) * (1.0 / (NZ * COLS))
        scale = lax.rsqrt(mean + 1e-05)
        gate = acc[here, :HID] * scale
        up = acc[here, HALF_N:HALF_N + HID] * scale
        inner[here, :] = (gate / (1.0 + jnp.exp(-gate)) * up).astype(BF16)

    def rs_copy(group, rel):
        _, _, off, rows, _ = groups[group]
        here = pl.ds(off, rows)
        at = (rel, group_sem[group])
        return remote(
            sib_out.at[rel, here], sib_in.at[rel, here], rs_send.at[at], rs_recv.at[at], sibling
        )

    def ry_copy(rel):
        return remote(y_out.at[rel], y_in.at[rel], ry_send.at[rel], ry_recv.at[rel], partner)

    def prepare(group, *rels):
        first, rows, off, count, _ = groups[group]
        for rel in rels:
            value = jnp.dot(
                inner[first:first + rows, :], down_v[slice_at(rel)], preferred_element_type=F32
            )
            step = CHUNK if group != "b" else SHARED
            for i in range(0, count, step):
                part[rel, off + i:off + i + step] = value[2 * i:2 * i + step]
                sib_out[rel, off + i:off + i + step] = value[2 * i + step:2 * (i + step)].astype(BF16)
            go(rs_copy(group, rel))

    def join(group, *rels):
        _, _, off, count, _ = groups[group]
        for rel in rels:
            rs_copy(group, rel).wait_recv()
            if group != "b":
                here = slice(off, off + count)
                part[rel, here] += sib_in[rel, here].astype(F32)
                continue
            other = rows_at(other_off, CHUNK)
            y_out[rel] = (part[rel, other] + sib_in[rel, other].astype(F32)).astype(BF16)
            go(ry_copy(rel))
            own = rows_at(own_off, CHUNK)
            part[rel, own] += sib_in[rel, own].astype(F32)

    def y_join(*rels):
        own = rows_at(own_off, CHUNK)
        for rel in rels:
            ry_copy(rel).wait_recv()
            part[rel, own] += y_in[rel].astype(F32)

    def ring_copy(way, distance, lane):
        piece = lanes[lane][way]
        first, rows = part_of(way, lane, distance)
        here = rows_at(piece_off[piece] + first, rows)
        at = (way, distance - 1, piece)
        return remote(
            ring_out.at[way, distance - 1, here], ring_in.at[way, distance - 1, here],
            r_send.at[at], r_recv.at[at], toward[way],
        )

    def incoming(way, distance, lane):
        ring_copy(way, distance, lane).wait_recv()
        first, rows = part_of(way, lane, distance)
        here = rows_at(piece_off[lanes[lane][way]] + first, rows)
        return ring_in[way, distance - 1, here].astype(F32)

    def ring(lane, distance):
        for way in (RIGHT, LEFT):
            first, rows = part_of(way, lane, distance)
            here = rows_at(piece_off[lanes[lane][way]] + first, rows)
            value = part[rel_of(way, distance), here]
            if distance < 3 or (distance == 3 and lane == "A0"):
                value = value + incoming(way, distance + 1, lane)
            elif distance == 3 and lane != "A1":
                arrived = incoming(way, 4, lane)
                if way == RIGHT:
                    value = jnp.concatenate([value[:HALF] + arrived, value[HALF:]], axis=0)
                else:
                    value = jnp.concatenate([value[:HALF], value[HALF:] + arrived], axis=0)
            ring_out[way, distance - 1, here] = value.astype(BF16)
            go(ring_copy(way, distance, lane))

    def send_back(q):
        sx, sy = seq_of(q)
        return remote(ret_out.at[q], ret.at[xy], b_send.at[q], b_recv.at[xy], plane(sx, sy))

    def is_me(q):
        sx, sy = seq_of(q)
        return (sx == x) & (sy == y)

    def finish(piece):
        value = part[0, rows_at(piece_off[piece], CHUNK)]
        for way in (RIGHT, LEFT):
            lane = next(name for name in used if lanes[name][way] == piece)
            value = value + incoming(way, 1, lane)
        first = first_q[piece]
        ret_out[first:first + 4] = jnp.concatenate(
            [value[:, :WIDE].reshape(4, CAP, WIDE), value[:, WIDE:].reshape(4, CAP, WIDE)], axis=1
        ).astype(BF16)
        for q in range(first, first + 4):
            pl.when(jnp.logical_not(is_me(q)))(send_back(q).start)

    def drain():
        for copy in started:
            copy.wait_send()
        started.clear()

    used = ("B", "A0", "A1")
    start(OWN)
    first_hop("B")
    spread(0, OWN)
    start(C0)
    start(C1)
    first_hop("A0")
    spread(0, C0)
    spread(0, C1)
    stats(0)
    hop("B", 1)
    first_hop("A1")
    y_arrive(0)
    multiply("a", 0)
    hop("A0", 1)
    multiply("b", 0)
    hop("B", 2)
    y_arrive(1, 7)
    hop("A1", 1)
    stats(1)
    multiply("a", 1)
    hop("A0", 2)
    multiply("a", 7)
    hop("B", 3)
    multiply("b", 1)
    y_arrive(2, 6)
    hop("A1", 2)
    multiply("b", 7)
    stats(2)
    multiply("a", 2)
    hop("A0", 3)
    multiply("a", 6)
    hop("B", 4)
    y_arrive(3, 5)
    multiply("b", 2)
    hop("A1", 3)
    multiply("b", 6)
    multiply("a", 3)
    multiply("b", 3)
    hop("A0", 4)
    multiply("a", 5)
    multiply("a", 4)
    activate("a")
    prepare("a", 4)
    y_arrive(4)
    prepare("a", 3, 5)
    multiply("b", 5)
    join("a", 4)
    ring("A0", 4)
    multiply("b", 4)
    activate("b")
    prepare("b", 4)
    join("a", 3, 5)
    ring("A1", 3)
    prepare("b", 3, 5)
    join("b", 4, 3, 5)
    prepare("a", 2, 6)
    prepare("b", 2, 6)
    y_join(4)
    ring("B", 4)
    join("a", 2, 6)
    ring("A0", 3)
    join("b", 2, 6)
    y_join(3, 5)
    ring("B", 3)
    ring("A1", 2)
    prepare("a", 1, 7)
    prepare("b", 1, 7)
    join("a", 1, 7)
    ring("A0", 2)
    join("b", 1, 7)
    y_join(2, 6)
    ring("B", 2)
    ring("A1", 1)
    prepare("a", 0)
    prepare("b", 0)
    join("a", 0)
    ring("A0", 1)
    join("b", 0)
    y_join(1, 7)
    ring("B", 1)
    stats(3)
    y_join(0)
    finish(C0)
    finish(C1)
    finish(OWN)

    @pl.when(goes(y))
    def _():
        ret[xy] = ret_out[my_q]

    drain()
    for i in range(15):
        allowed_i, copy = send_block(i)
        pl.when(allowed_i)(copy.wait_send)
    for i in range(1, 4):
        stat_copy(i, 0).wait_send()
        stat_copy(i, 1).wait_send()
    stat_copy(0, 2).wait_send()

    place = lax.broadcasted_iota(jnp.int32, (TOK, 16 * 2 * CAP), 1).astype(F32)
    spot = label_col * (4 * CAP) + rank_col
    take = [
        ((place == spot + half * CAP) | (place == spot + (2 + half) * CAP)).astype(BF16)
        for half in range(2)
    ]
    for i in range(16):
        arrival = remote(
            ret_out.at[0], ret.at[i], b_send.at[0], b_recv.at[i], plane(i // 4, i % 4)
        )
        pl.when(goes(i % 4) & (xy != i))(arrival.wait_recv)
    returned = ret[...].reshape(16 * 2 * CAP, WIDE)
    for half in range(2):
        cut = slice(half * WIDE, (half + 1) * WIDE)
        expert_out = jnp.dot(take[half], returned, preferred_element_type=F32)
        mixed_ref[:, cut] = (hidden[:, cut].astype(F32) + expert_out).astype(BF16)
    for q in range(12):
        pl.when(jnp.logical_not(is_me(q)))(send_back(q).wait_send)


def body(
    residual, queries, key_rows, value_rows, lengths, labels, losses, prior_weights, norm_gain,
    gate_weight, up_weight, down_weight,
):
    vmem = pl.BlockSpec(memory_space=pltpu.VMEM)
    smem = pl.BlockSpec(memory_space=pltpu.SMEM)
    hbm = pl.BlockSpec(memory_space=pl.ANY)
    dma = pltpu.SemaphoreType.DMA
    tile = (TOK, COLS)
    mixed, weights = pl.pallas_call(
        kernel,
        out_shape=(
            jax.ShapeDtypeStruct(tile, BF16),
            jax.ShapeDtypeStruct((1, EXPERTS), F32),
        ),
        in_specs=[smem, vmem, vmem, vmem, vmem] + [hbm] * 7,
        out_specs=(vmem, vmem),
        scratch_shapes=[
            pltpu.VMEM(tile, BF16),
            pltpu.VMEM(tile, BF16),
            pltpu.VMEM(tile, BF16),
            pltpu.VMEM(tile, BF16),
            pltpu.VMEM((HID, NZ * COLS), BF16),
            pltpu.VMEM((HID, NZ * COLS), BF16),
            pltpu.VMEM((NZ, HID, COLS), BF16),
            pltpu.VMEM((NZ * COLS, 2 * HALF_N), BF16),
            pltpu.VMEM(tile, BF16),
            pltpu.VMEM((EXPERTS, 2 * CAP, WIDE), BF16),
            pltpu.VMEM((12, 2 * CAP, WIDE), BF16),
            pltpu.VMEM((NZ, ROWS, COLS), BF16),
            pltpu.VMEM((ROWS, 2 * HALF_N), F32),
            pltpu.VMEM((ROWS, 128), F32),
            pltpu.VMEM((ROWS, HID), BF16),
            pltpu.VMEM((NZ, CORE_ROWS, COLS), F32),
            pltpu.VMEM((NZ, CORE_ROWS, COLS), BF16),
            pltpu.VMEM((NZ, CORE_ROWS, COLS), BF16),
            pltpu.VMEM((2, 4, CORE_ROWS, COLS), BF16),
            pltpu.VMEM((2, 4, CORE_ROWS, COLS), BF16),
            pltpu.VMEM((NZ, CHUNK, COLS), BF16),
            pltpu.VMEM((NZ, CHUNK, COLS), BF16),
            pltpu.VMEM((12, 2 * CAP, WIDE), BF16),
            pltpu.VMEM((16, 2 * CAP, WIDE), BF16),
            pltpu.VMEM((4, EXPERTS, 128), F32),
            pltpu.VMEM((4, EXPERTS, 128), F32),
            pltpu.VMEM((EXPERTS, 128), F32),
            pltpu.VMEM((3, EXPERTS, 128), F32),
            dma((4,)), dma((2 + NZ,)),
            dma((15,)), dma((12,)),
            dma((2, 4, 3)), dma((2, 4, 3)),
            dma((NZ, 4)), dma((NZ, 4)),
            dma((NZ,)), dma((NZ,)),
            dma((NZ, 3)), dma((NZ, 3)),
            dma((NZ,)), dma((NZ,)),
            dma((2, 4, 3)), dma((2, 4, 3)),
            dma((12,)), dma((16,)),
            dma((7,)), dma((9,)),
        ],
        compiler_params=pltpu.CompilerParams(
            collective_id=0, has_side_effects=True, vmem_limit_bytes=60 * 1024 * 1024
        ),
    )(
        lengths, labels.reshape(1, TOK), losses.reshape(1, TOK), prior_weights.reshape(1, EXPERTS),
        norm_gain.reshape(1, NZ * COLS), residual, queries, key_rows, value_rows,
        gate_weight.T, up_weight.T, down_weight,
    )
    return (mixed, weights.reshape(EXPERTS))


def solution(mesh):
    placed = (
        P("dp", "mp"),
        P("dp", "mp"),
        P("dp", "mp"),
        P("dp", "mp"),
        P("dp", None),
        P("dp", None),
        P("dp"),
        P(),
        P(),
        P(None, ("dp", "mp")),
        P(None, ("dp", "mp")),
        P(("dp", "mp"), None),
    )
    return jax.shard_map(
        body, mesh=mesh, in_specs=placed, out_specs=(P("dp", "mp"), P()), check_vma=False
    )
```

```python
import jax
import jax.numpy as jnp
from jax import lax
from jax.experimental import pallas as pl
from jax.experimental.pallas import tpu as pltpu
from jax.sharding import PartitionSpec as P

HEAD_DIM = 128
EXPERTS = 8
CAP = 24
TOK = 128
COLS = 512
HID = 344
HALF_N = 384
NZ = 8
CORE_ROWS = 16 * CAP
ROWS = 2 * CORE_ROWS
CHUNK = 4 * CAP
HALF = CHUNK // 2
WIDE = COLS // 2
SHARED = 2 * CHUNK
RIGHT, LEFT = 0, 1
F32, BF16 = jnp.float32, jnp.bfloat16
MESH = pl.DeviceIdType.MESH
NT = (((1,), (1,)), ((), ()))

dro_step = 0.5


def kernel(
    lengths_hbm, labels_hbm, losses_hbm, prior_hbm, gain_hbm,
    res_hbm, q_hbm, k_hbm, v_hbm, gate_hbm, up_hbm, down_hbm,
    mixed_ref, weights_ref,
    lengths_ref, labels_ref, losses_ref, prior_ref, gain_ref,
    res_v, q_v, k_v, v_v, gate_v, up_v, down_v, both_v,
    hidden, packed, stage, xb, acc, square, inner,
    part, sib_out, sib_in, ring_in, ring_out, y_out, y_in, ret_out, ret,
    stat_x, stat_y, stat_c, stat_src,
    in_sem, w_sem, a_send, a_recv, g_send, g_recv, gs_send, gs_recv, gy_send, gy_recv,
    rs_send, rs_recv, ry_send, ry_recv, r_send, r_recv, b_send, b_recv, st_send, st_recv,
):
    dp = lax.axis_index("dp")
    z = lax.axis_index("mp")
    core = lax.rem(dp, 2)
    xy = dp // 2
    x, y = xy // 4, lax.rem(xy, 4)
    yb = lax.rem(y, 2)

    def plane(tx, ty, tc=None):
        return ((tx * 4 + ty) * 2 + (core if tc is None else tc), z)

    sibling = (dp + 1 - 2 * core, z)
    partner = plane(x, y + 1 - 2 * yb)
    z_right = (dp, lax.rem(z + 1, NZ))
    z_left = (dp, lax.rem(z + NZ - 1, NZ))
    toward = (z_right, z_left)
    offsets = sorted(
        ((i // 4, i % 4) for i in range(1, 16)),
        key=lambda o: -(min(o[0], 4 - o[0]) + min(o[1], 4 - o[1])),
    )

    barrier = pltpu.get_barrier_semaphore()
    peers = [plane(lax.rem(x + dx, 4), lax.rem(y + dy, 4)) for dx, dy in offsets]
    peers += [sibling, z_right, z_left]
    for peer in peers:
        pl.semaphore_signal(barrier, inc=1, device_id=peer, device_id_type=MESH)

    loads = [
        pltpu.make_async_copy(src, dst, in_sem.at[i])
        for i, (src, dst) in enumerate((
            (labels_hbm, labels_ref), (lengths_hbm, lengths_ref), (losses_hbm, losses_ref),
            (q_hbm, q_v), (k_hbm, k_v), (v_hbm, v_v), (res_hbm, res_v),
            (prior_hbm, prior_ref), (gain_hbm, gain_ref),
        ))
    ]
    for load in loads:
        load.start()
    weight_loads = [
        pltpu.make_async_copy(gate_hbm, gate_v, w_sem.at[0]),
        pltpu.make_async_copy(up_hbm, up_v, w_sem.at[1]),
    ] + [
        pltpu.make_async_copy(down_hbm.at[:, pl.ds(i * COLS, COLS)], down_v.at[i], w_sem.at[2 + i])
        for i in range(NZ)
    ]
    for load in weight_loads:
        load.start()

    def remote(src, dst, send, recv, device):
        return pltpu.make_async_remote_copy(
            src_ref=src, dst_ref=dst, send_sem=send, recv_sem=recv,
            device_id=device, device_id_type=MESH,
        )

    for load in loads:
        load.wait()

    at0 = lax.broadcasted_iota(jnp.int32, (TOK, TOK), 0)
    at1 = lax.broadcasted_iota(jnp.int32, (TOK, TOK), 1)
    label_row = labels_ref[...].astype(F32)
    label_col = jnp.sum(jnp.where(at0 == at1, label_row, 0.0), axis=1, keepdims=True)
    same = label_col == label_row
    rank_row = jnp.sum(jnp.where(same & (at0 < at1), 1.0, 0.0), axis=0, keepdims=True)
    rank_col = jnp.sum(jnp.where(same & (at1 < at0), 1.0, 0.0), axis=1, keepdims=True)
    slot_row = label_row * (2 * CAP) + rank_row
    slot_ids = lax.broadcasted_iota(jnp.int32, (EXPERTS * 2 * CAP, TOK), 0).astype(F32)
    select = [(slot_ids == slot_row + half * CAP).astype(BF16) for half in range(2)]

    domain = lax.broadcasted_iota(jnp.int32, (EXPERTS, TOK), 0).astype(F32)
    lane = lax.broadcasted_iota(jnp.int32, (EXPERTS, TOK), 1)
    member = (domain == label_row).astype(F32)
    loss_sum = jnp.sum(member * losses_ref[...], axis=1, keepdims=True)
    count = jnp.sum(member, axis=1, keepdims=True)
    stat_src[0] = jnp.where(lane == 0, loss_sum, jnp.where(lane == 1, count, 0.0))

    ends = [lengths_ref[0, 0]]
    for i in range(1, 4):
        ends.append(ends[-1] + lengths_ref[0, i])
    doc0 = sum((at0 >= end).astype(jnp.int32) for end in ends)
    doc1 = sum((at1 >= end).astype(jnp.int32) for end in ends)
    allowed = (doc0 == doc1) & (at1 <= at0)
    for head in range(COLS // HEAD_DIM):
        cut = slice(head * HEAD_DIM, (head + 1) * HEAD_DIM)
        scores = lax.dot_general(
            q_v[:, cut], k_v[:, cut], NT, preferred_element_type=F32
        ) * HEAD_DIM ** (-0.5)
        scores = jnp.where(allowed, scores, -1e30)
        exp_scores = jnp.exp(scores - jnp.max(scores, axis=1, keepdims=True))
        probs = (exp_scores / jnp.sum(exp_scores, axis=1, keepdims=True)).astype(BF16)
        attn = jnp.dot(probs, v_v[:, cut], preferred_element_type=F32)
        hidden[:, cut] = (res_v[:, cut].astype(F32) + attn).astype(BF16)
    packed[...] = (
        (
            jnp.dot(select[0], hidden[:, :WIDE], preferred_element_type=F32)
            + jnp.dot(select[1], hidden[:, WIDE:], preferred_element_type=F32)
        )
        .astype(BF16)
        .reshape(EXPERTS, 2 * CAP, WIDE)
    )

    pl.semaphore_wait(barrier, len(peers))

    kind = lax.rem(x + y, 4)
    my_q = jnp.where(kind >= 2, (kind - 2) * 4 + y, 8 + y)

    def goes(ty):
        return (kind >= 2) | (lax.rem(ty, 2) == kind)

    def send_block(i):
        dx, dy = offsets[i]
        tx, ty = lax.rem(x + dx, 4), lax.rem(y + dy, 4)
        copy = remote(
            packed.at[2 * tx + ty // 2], stage.at[my_q], a_send.at[i], a_recv.at[my_q], plane(tx, ty)
        )
        return goes(ty), copy

    for i in range(15):
        allowed_i, copy = send_block(i)
        pl.when(allowed_i)(copy.start)

    @pl.when(goes(y))
    def _():
        stage[my_q] = packed[2 * x + y // 2]

    def seq_of(q):
        sy = q % 4
        if q < 8:
            return (2 + q // 4 - sy) % 4, sy
        return lax.rem(yb - sy + 4, 4), sy

    def stat_copy(i, phase):
        if phase == 0:
            dst, peer = stat_x, plane(lax.rem(x + i, 4), y)
            return remote(stat_src.at[0], dst.at[x], st_send.at[i - 1], st_recv.at[x], peer)
        if phase == 1:
            dst, peer = stat_y, plane(x, lax.rem(y + i, 4))
            return remote(stat_src.at[1], dst.at[y], st_send.at[2 + i], st_recv.at[4 + y], peer)
        return remote(stat_src.at[2], stat_c, st_send.at[6], st_recv.at[8], sibling)

    def stat_wait(i, phase):
        if phase == 0:
            at = lax.rem(x + i, 4)
            return remote(stat_src.at[0], stat_x.at[at], st_send.at[0], st_recv.at[at], plane(at, y))
        at = lax.rem(y + i, 4)
        return remote(stat_src.at[1], stat_y.at[at], st_send.at[0], st_recv.at[4 + at], plane(x, at))

    def stats(step):
        if step == 0:
            for i in range(1, 4):
                stat_copy(i, 0).start()
            stat_x[x] = stat_src[0]
        elif step == 1:
            for i in range(1, 4):
                stat_wait(i, 0).wait_recv()
            stat_src[1] = (stat_x[0] + stat_x[1]) + (stat_x[2] + stat_x[3])
            for i in range(1, 4):
                stat_copy(i, 1).start()
            stat_y[y] = stat_src[1]
        elif step == 2:
            for i in range(1, 4):
                stat_wait(i, 1).wait_recv()
            stat_src[2] = (stat_y[0] + stat_y[1]) + (stat_y[2] + stat_y[3])
            stat_copy(0, 2).start()
        else:
            stat_copy(0, 2).wait_recv()
            totals = stat_src[2] + stat_c[...]
            domain_mean = totals[:, 0:1] / totals[:, 1:2]
            eye = lax.broadcasted_iota(jnp.int32, (EXPERTS, EXPERTS), 0) == lax.broadcasted_iota(
                jnp.int32, (EXPERTS, EXPERTS), 1
            )
            mean_row = jnp.sum(jnp.where(eye, domain_mean, 0.0), axis=0, keepdims=True)
            scaled = prior_ref[...] * jnp.exp(dro_step * mean_row)
            weights_ref[...] = EXPERTS * scaled / jnp.sum(scaled, axis=1, keepdims=True)

    acc[...] = jnp.zeros_like(acc)
    square[...] = jnp.zeros_like(square)
    for i in range(16):
        @pl.when(jnp.logical_not(goes(i % 4)))
        def _():
            ret[i] = jnp.zeros((2 * CAP, WIDE), BF16)

    for load in weight_loads:
        load.wait()

    def turn(i, carry):
        at = pl.ds(pl.multiple_of(i * COLS, COLS), COLS)
        for half, source in enumerate((gate_v, up_v)):
            first = half * HALF_N
            both_v[at, first + HALF_N - 128:first + HALF_N] = jnp.zeros((COLS, 128), BF16)
            both_v[at, first:first + HID] = source[:, at].T
        return carry

    lax.fori_loop(0, NZ, turn, 0)

    own_off = SHARED + yb * CHUNK
    other_off = SHARED + (1 - yb) * CHUNK
    OWN, C0, C1, OTHER = 0, 1, 2, 3
    piece_off = (own_off, 0, CHUNK, other_off)
    b_first = 2 * SHARED
    own_at = (b_first + yb * CHUNK, 0, CHUNK, b_first + (1 - yb) * CHUNK)
    groups = {"a": (0, 0, 0), "b": (b_first, SHARED, 1)}
    lanes = {"B": (OWN, OWN), "A0": (C0, C1), "A1": (C1, C0)}
    first_q = {C0: 0, C1: 4, OWN: 8}

    def slice_at(rel):
        return lax.rem(z + rel, NZ)

    def rel_of(way, distance):
        return distance if way == RIGHT else (NZ - distance) % NZ

    def rows_at(off, rows):
        if isinstance(off, int):
            return pl.ds(off, rows)
        return pl.ds(pl.multiple_of(off, 16), rows)

    def part_of(way, lane, distance):
        if distance < 4 or lane in ("A0", "A1"):
            return 0, CHUNK
        return way * HALF, HALF

    started = []

    def go(copy):
        copy.start()
        started.append(copy)

    def gather_copy(way, hop, lane, sending):
        rel = rel_of(1 - way, hop - 1 if sending else hop)
        piece = lanes[lane][way]
        first, rows = part_of(way, lane, hop)
        ref = xb.at[slice_at(rel), rows_at(own_at[piece] + first, rows)]
        at = (way, hop - 1, piece)
        return remote(ref, ref, g_send.at[at], g_recv.at[at], toward[way])

    def sib_copy(group, rel):
        first, _, number = groups[group]
        rows = xb.at[slice_at(rel)]
        return remote(
            rows.at[pl.ds(first, SHARED)], rows.at[pl.ds(first + SHARED, SHARED)],
            gs_send.at[rel, number], gs_recv.at[rel, number], sibling,
        )

    def share(group, rel):
        go(sib_copy(group, rel))

    def y_copy(rel, mine=True):
        ref = xb.at[slice_at(rel), rows_at(own_at[OWN if mine else OTHER], CHUNK)]
        return remote(ref, ref, gy_send.at[rel], gy_recv.at[rel], partner)

    def spread(rel, piece):
        if piece == OWN:
            go(y_copy(rel))

    def start(piece):
        first = first_q[piece]
        for q in range(first, first + 4):
            sx, sy = seq_of(q)
            arrival = remote(
                packed.at[0], stage.at[q], a_send.at[0], a_recv.at[q], plane(sx, sy)
            )
            pl.when((sx != x) | (sy != y))(arrival.wait_recv)
        blocks = stage[first:first + 4].astype(F32)
        here = rows_at(own_at[piece], CHUNK)
        for half in range(2):
            xb[z, here, half * WIDE:(half + 1) * WIDE] = (
                blocks[:, half * CAP:(half + 1) * CAP].reshape(CHUNK, WIDE).astype(BF16)
            )

    def first_hop(lane):
        for way in (RIGHT, LEFT):
            go(gather_copy(way, 1, lane, True))

    def own_spread(piece):
        spread(0, piece)

    def hop(lane, h):
        for way in (RIGHT, LEFT):
            gather_copy(way, h, lane, False).wait_recv()
            if h < 3 or (h == 3 and lane != "A1"):
                go(gather_copy(way, h + 1, lane, True))
        first, second = lanes[lane]
        if h == 4 and first == second:
            spread(4, first)
            return
        for way in (RIGHT, LEFT):
            spread(rel_of(1 - way, h), lanes[lane][way])

    def y_arrive(*rels):
        for rel in rels:
            y_copy(rel, mine=False).wait_recv()
            share("b", rel)

    def multiply(group, *rels):
        here = pl.ds(groups[group][0], 2 * SHARED)
        for rel in rels:
            sib_copy(group, rel).wait_recv()
            s = slice_at(rel)
            at = pl.ds(pl.multiple_of(s * COLS, COLS), COLS)
            value = xb[s, here, :].astype(F32)
            sq = value * value
            square[here, :] += sq[:, :128] + sq[:, 128:256] + sq[:, 256:384] + sq[:, 384:]
            scaled = (value * gain_ref[:, at]).astype(BF16)
            acc[here, :] += jnp.dot(scaled, both_v[at, :], preferred_element_type=F32)

    def activate(group):
        here = pl.ds(groups[group][0], 2 * SHARED)
        mean = jnp.sum(square[here, :], axis=1, keepdims=True) * (1.0 / (NZ * COLS))
        scale = lax.rsqrt(mean + 1e-05)
        gate = acc[here, :HID] * scale
        up = acc[here, HALF_N:HALF_N + HID] * scale
        inner[here, :] = (gate / (1.0 + jnp.exp(-gate)) * up).astype(BF16)

    def rs_copy(group, rel):
        _, off, number = groups[group]
        here = pl.ds(off, SHARED)
        at = (rel, number)
        return remote(
            sib_out.at[rel, here], sib_in.at[rel, here], rs_send.at[at], rs_recv.at[at], sibling
        )

    def ry_copy(rel):
        return remote(y_out.at[rel], y_in.at[rel], ry_send.at[rel], ry_recv.at[rel], partner)

    def prepare(group, *rels):
        first, off, _ = groups[group]
        for rel in rels:
            value = jnp.dot(
                inner[first:first + 2 * SHARED, :], down_v[slice_at(rel)], preferred_element_type=F32
            )
            sib_out[rel, off:off + SHARED] = value[SHARED:].astype(BF16)
            part[rel, off:off + SHARED] = value[:SHARED]
            go(rs_copy(group, rel))

    def join(group, *rels):
        for rel in rels:
            rs_copy(group, rel).wait_recv()
            if group == "a":
                part[rel, :SHARED] += sib_in[rel, :SHARED].astype(F32)
                continue
            other = rows_at(other_off, CHUNK)
            y_out[rel] = (part[rel, other] + sib_in[rel, other].astype(F32)).astype(BF16)
            go(ry_copy(rel))
            own = rows_at(own_off, CHUNK)
            part[rel, own] += sib_in[rel, own].astype(F32)

    def y_join(*rels):
        own = rows_at(own_off, CHUNK)
        for rel in rels:
            ry_copy(rel).wait_recv()
            part[rel, own] += y_in[rel].astype(F32)

    def ring_copy(way, distance, lane):
        piece = lanes[lane][way]
        first, rows = part_of(way, lane, distance)
        here = rows_at(piece_off[piece] + first, rows)
        at = (way, distance - 1, piece)
        return remote(
            ring_out.at[way, distance - 1, here], ring_in.at[way, distance - 1, here],
            r_send.at[at], r_recv.at[at], toward[way],
        )

    def incoming(way, distance, lane):
        ring_copy(way, distance, lane).wait_recv()
        first, rows = part_of(way, lane, distance)
        here = rows_at(piece_off[lanes[lane][way]] + first, rows)
        return ring_in[way, distance - 1, here].astype(F32)

    def ring(lane, distance):
        for way in (RIGHT, LEFT):
            first, rows = part_of(way, lane, distance)
            here = rows_at(piece_off[lanes[lane][way]] + first, rows)
            value = part[rel_of(way, distance), here]
            if distance < 3 or (distance == 3 and lane == "A0"):
                value = value + incoming(way, distance + 1, lane)
            elif distance == 3 and lane != "A1":
                arrived = incoming(way, 4, lane)
                if way == RIGHT:
                    value = jnp.concatenate([value[:HALF] + arrived, value[HALF:]], axis=0)
                else:
                    value = jnp.concatenate([value[:HALF], value[HALF:] + arrived], axis=0)
            ring_out[way, distance - 1, here] = value.astype(BF16)
            go(ring_copy(way, distance, lane))

    def send_back(q):
        sx, sy = seq_of(q)
        return remote(ret_out.at[q], ret.at[xy], b_send.at[q], b_recv.at[xy], plane(sx, sy))

    def is_me(q):
        sx, sy = seq_of(q)
        return (sx == x) & (sy == y)

    def finish(piece):
        value = part[0, rows_at(piece_off[piece], CHUNK)]
        for way in (RIGHT, LEFT):
            lane = next(name for name in used if lanes[name][way] == piece)
            value = value + incoming(way, 1, lane)
        first = first_q[piece]
        ret_out[first:first + 4] = jnp.concatenate(
            [value[:, :WIDE].reshape(4, CAP, WIDE), value[:, WIDE:].reshape(4, CAP, WIDE)], axis=1
        ).astype(BF16)
        for q in range(first, first + 4):
            pl.when(jnp.logical_not(is_me(q)))(send_back(q).start)

    def drain():
        for copy in started:
            copy.wait_send()
        started.clear()

    used = ("B", "A0", "A1")
    start(OWN)
    spread(0, OWN)
    first_hop("B")
    start(C0)
    spread(0, C0)
    start(C1)
    spread(0, C1)
    first_hop("A0")
    share("a", 0)
    first_hop("A1")
    multiply("a", 0)
    y_arrive(0)
    hop("B", 1)
    stats(0)
    multiply("b", 0)
    hop("A0", 1)
    hop("A1", 1)
    share("a", 1)
    share("a", 7)
    multiply("a", 1)
    hop("B", 2)
    stats(1)
    multiply("a", 7)
    y_arrive(1, 7)
    hop("A0", 2)
    multiply("b", 1)
    multiply("b", 7)
    hop("A1", 2)
    share("a", 2)
    share("a", 6)
    multiply("a", 2)
    hop("B", 3)
    multiply("a", 6)
    y_arrive(2, 6)
    hop("A0", 3)
    multiply("b", 2)
    multiply("b", 6)
    hop("A1", 3)
    share("a", 5)
    share("a", 3)
    hop("B", 4)
    stats(2)
    multiply("a", 5)
    multiply("a", 3)
    hop("A0", 4)
    share("a", 4)
    y_arrive(3, 5)
    multiply("a", 4)
    activate("a")
    prepare("a", 3)
    y_arrive(4)
    prepare("a", 4)
    multiply("b", 3)
    multiply("b", 5)
    multiply("b", 4)
    activate("b")
    prepare("b", 4)
    prepare("b", 6)
    join("a", 3)
    prepare("b", 3)
    join("a", 4)
    join("b", 4)
    ring("A0", 4)
    prepare("a", 5)
    join("b", 3)
    prepare("a", 7)
    prepare("b", 5)
    join("a", 5)
    ring("A1", 3)
    prepare("a", 6)
    join("a", 7)
    join("b", 5)
    prepare("a", 2)
    join("b", 6)
    y_join(4)
    ring("B", 4)
    ring("A0", 3)
    join("a", 2)
    prepare("b", 7)
    prepare("b", 2)
    prepare("a", 0)
    join("a", 6)
    ring("A1", 2)
    join("b", 7)
    join("b", 2)
    y_join(5)
    join("a", 0)
    y_join(3)
    ring("B", 3)
    prepare("a", 1)
    prepare("b", 0)
    y_join(6)
    prepare("b", 1)
    ring("A0", 2)
    join("a", 1)
    join("b", 0)
    join("b", 1)
    ring("A1", 1)
    y_join(7)
    y_join(2)
    ring("B", 2)
    ring("A0", 1)
    y_join(0)
    y_join(1)
    ring("B", 1)
    stats(3)
    finish(C1)
    finish(C0)
    finish(OWN)

    @pl.when(goes(y))
    def _():
        ret[xy] = ret_out[my_q]

    drain()
    for i in range(15):
        allowed_i, copy = send_block(i)
        pl.when(allowed_i)(copy.wait_send)
    for i in range(1, 4):
        stat_copy(i, 0).wait_send()
        stat_copy(i, 1).wait_send()
    stat_copy(0, 2).wait_send()

    place = lax.broadcasted_iota(jnp.int32, (TOK, 16 * 2 * CAP), 1).astype(F32)
    spot = label_col * (4 * CAP) + rank_col
    take = [
        ((place == spot + half * CAP) | (place == spot + (2 + half) * CAP)).astype(BF16)
        for half in range(2)
    ]
    for i in range(16):
        arrival = remote(
            ret_out.at[0], ret.at[i], b_send.at[0], b_recv.at[i], plane(i // 4, i % 4)
        )
        pl.when(goes(i % 4) & (xy != i))(arrival.wait_recv)
    returned = ret[...].reshape(16 * 2 * CAP, WIDE)
    for half in range(2):
        cut = slice(half * WIDE, (half + 1) * WIDE)
        expert_out = jnp.dot(take[half], returned, preferred_element_type=F32)
        mixed_ref[:, cut] = (hidden[:, cut].astype(F32) + expert_out).astype(BF16)
    for q in range(12):
        pl.when(jnp.logical_not(is_me(q)))(send_back(q).wait_send)


def hand_on(mixed_in, weights_in, mixed_out, weights_out):
    mixed_out[...] = mixed_in[...]
    weights_out[...] = weights_in[...]


def body(
    residual, queries, key_rows, value_rows, lengths, labels, losses, prior_weights, norm_gain,
    gate_weight, up_weight, down_weight,
):
    vmem = pl.BlockSpec(memory_space=pltpu.VMEM)
    hbm = pl.BlockSpec(memory_space=pl.ANY)
    dma = pltpu.SemaphoreType.DMA
    tile = (TOK, COLS)
    mixed, weights = pl.pallas_call(
        kernel,
        out_shape=(
            jax.ShapeDtypeStruct(tile, BF16),
            jax.ShapeDtypeStruct((1, EXPERTS), F32),
        ),
        in_specs=[hbm] * 12,
        out_specs=(vmem, vmem),
        scratch_shapes=[
            pltpu.SMEM((1, 4), jnp.int32),
            pltpu.VMEM((1, TOK), jnp.int32),
            pltpu.VMEM((1, TOK), F32),
            pltpu.VMEM((1, EXPERTS), F32),
            pltpu.VMEM((1, NZ * COLS), F32),
            pltpu.VMEM(tile, BF16),
            pltpu.VMEM(tile, BF16),
            pltpu.VMEM(tile, BF16),
            pltpu.VMEM(tile, BF16),
            pltpu.VMEM((HID, NZ * COLS), BF16),
            pltpu.VMEM((HID, NZ * COLS), BF16),
            pltpu.VMEM((NZ, HID, COLS), BF16),
            pltpu.VMEM((NZ * COLS, 2 * HALF_N), BF16),
            pltpu.VMEM(tile, BF16),
            pltpu.VMEM((EXPERTS, 2 * CAP, WIDE), BF16),
            pltpu.VMEM((12, 2 * CAP, WIDE), BF16),
            pltpu.VMEM((NZ, ROWS, COLS), BF16),
            pltpu.VMEM((ROWS, 2 * HALF_N), F32),
            pltpu.VMEM((ROWS, 128), F32),
            pltpu.VMEM((ROWS, HID), BF16),
            pltpu.VMEM((NZ, CORE_ROWS, COLS), F32),
            pltpu.VMEM((NZ, CORE_ROWS, COLS), BF16),
            pltpu.VMEM((NZ, CORE_ROWS, COLS), BF16),
            pltpu.VMEM((2, 4, CORE_ROWS, COLS), BF16),
            pltpu.VMEM((2, 4, CORE_ROWS, COLS), BF16),
            pltpu.VMEM((NZ, CHUNK, COLS), BF16),
            pltpu.VMEM((NZ, CHUNK, COLS), BF16),
            pltpu.VMEM((12, 2 * CAP, WIDE), BF16),
            pltpu.VMEM((16, 2 * CAP, WIDE), BF16),
            pltpu.VMEM((4, EXPERTS, 128), F32),
            pltpu.VMEM((4, EXPERTS, 128), F32),
            pltpu.VMEM((EXPERTS, 128), F32),
            pltpu.VMEM((3, EXPERTS, 128), F32),
            dma((9,)), dma((2 + NZ,)),
            dma((15,)), dma((12,)),
            dma((2, 4, 3)), dma((2, 4, 3)),
            dma((NZ, 2)), dma((NZ, 2)),
            dma((NZ,)), dma((NZ,)),
            dma((NZ, 2)), dma((NZ, 2)),
            dma((NZ,)), dma((NZ,)),
            dma((2, 4, 3)), dma((2, 4, 3)),
            dma((12,)), dma((16,)),
            dma((7,)), dma((9,)),
        ],
        compiler_params=pltpu.CompilerParams(
            collective_id=0, has_side_effects=True, vmem_limit_bytes=60 * 1024 * 1024
        ),
    )(
        lengths, labels.reshape(1, TOK), losses.reshape(1, TOK), prior_weights.reshape(1, EXPERTS),
        norm_gain.reshape(1, NZ * COLS), residual, queries, key_rows, value_rows,
        gate_weight.T, up_weight.T, down_weight,
    )
    mixed, weights = pl.pallas_call(
        hand_on,
        out_shape=(
            jax.ShapeDtypeStruct(tile, BF16),
            jax.ShapeDtypeStruct((1, EXPERTS), F32),
        ),
        in_specs=[vmem, vmem],
        out_specs=(vmem, vmem),
    )(mixed, weights)
    return (mixed, weights.reshape(EXPERTS))


def solution(mesh):
    placed = (
        P("dp", "mp"),
        P("dp", "mp"),
        P("dp", "mp"),
        P("dp", "mp"),
        P("dp", None),
        P("dp", None),
        P("dp"),
        P(),
        P(),
        P(None, ("dp", "mp")),
        P(None, ("dp", "mp")),
        P(("dp", "mp"), None),
    )
    return jax.shard_map(
        body, mesh=mesh, in_specs=placed, out_specs=(P("dp", "mp"), P()), check_vma=False
    )
```

```python
import jax
import jax.numpy as jnp
from jax import lax
from jax.experimental import pallas as pl
from jax.experimental.pallas import tpu as pltpu
from jax.sharding import PartitionSpec as P

HEAD_DIM = 128
EXPERTS = 8
CAP = 24
TOK = 128
COLS = 512
HID = 344
HALF_N = 384
NZ = 8
CORE_ROWS = 16 * CAP
ROWS = 2 * CORE_ROWS
CHUNK = 4 * CAP
HALF = CHUNK // 2
WIDE = COLS // 2
SHARED = 2 * CHUNK
RIGHT, LEFT = 0, 1
F32, BF16 = jnp.float32, jnp.bfloat16
MESH = pl.DeviceIdType.MESH
NT = (((1,), (1,)), ((), ()))

dro_step = 0.5


def kernel(
    lengths_hbm, labels_hbm, losses_hbm, prior_hbm, gain_hbm,
    res_hbm, q_hbm, k_hbm, v_hbm, gate_hbm, up_hbm, down_hbm,
    mixed_ref, weights_ref,
    lengths_ref, labels_ref, losses_ref, prior_ref, gain_ref,
    res_v, q_v, k_v, v_v, gate_v, up_v, down_v, both_v,
    hidden, packed, stage, xb, acc, square, inner,
    part, sib_out, sib_in, ring_in, ring_out, y_out, y_in, ret_out, ret,
    stat_x, stat_y, stat_c, stat_src,
    in_sem, w_sem, a_send, a_recv, g_send, g_recv, gs_send, gs_recv, gy_send, gy_recv,
    rs_send, rs_recv, ry_send, ry_recv, r_send, r_recv, b_send, b_recv, st_send, st_recv,
):
    dp = lax.axis_index("dp")
    z = lax.axis_index("mp")
    core = lax.rem(dp, 2)
    xy = dp // 2
    x, y = xy // 4, lax.rem(xy, 4)
    yb = lax.rem(y, 2)

    def plane(tx, ty, tc=None):
        return ((tx * 4 + ty) * 2 + (core if tc is None else tc), z)

    sibling = (dp + 1 - 2 * core, z)
    partner = plane(x, y + 1 - 2 * yb)
    z_right = (dp, lax.rem(z + 1, NZ))
    z_left = (dp, lax.rem(z + NZ - 1, NZ))
    toward = (z_right, z_left)
    offsets = sorted(
        ((i // 4, i % 4) for i in range(1, 16)),
        key=lambda o: -(min(o[0], 4 - o[0]) + min(o[1], 4 - o[1])),
    )

    barrier = pltpu.get_barrier_semaphore()
    peers = [plane(lax.rem(x + dx, 4), lax.rem(y + dy, 4)) for dx, dy in offsets]
    peers += [sibling, z_right, z_left]
    for peer in peers:
        pl.semaphore_signal(barrier, inc=1, device_id=peer, device_id_type=MESH)

    loads = [
        pltpu.make_async_copy(src, dst, in_sem.at[i])
        for i, (src, dst) in enumerate((
            (labels_hbm, labels_ref), (lengths_hbm, lengths_ref), (losses_hbm, losses_ref),
            (q_hbm, q_v), (k_hbm, k_v), (v_hbm, v_v), (res_hbm, res_v),
            (prior_hbm, prior_ref), (gain_hbm, gain_ref),
        ))
    ]
    for load in loads:
        load.start()
    weight_loads = [
        pltpu.make_async_copy(gate_hbm, gate_v, w_sem.at[0]),
        pltpu.make_async_copy(up_hbm, up_v, w_sem.at[1]),
    ] + [
        pltpu.make_async_copy(down_hbm.at[:, pl.ds(i * COLS, COLS)], down_v.at[i], w_sem.at[2 + i])
        for i in range(NZ)
    ]
    for load in weight_loads:
        load.start()

    def remote(src, dst, send, recv, device):
        return pltpu.make_async_remote_copy(
            src_ref=src, dst_ref=dst, send_sem=send, recv_sem=recv,
            device_id=device, device_id_type=MESH,
        )

    for load in loads:
        load.wait()

    at0 = lax.broadcasted_iota(jnp.int32, (TOK, TOK), 0)
    at1 = lax.broadcasted_iota(jnp.int32, (TOK, TOK), 1)
    label_row = labels_ref[...].astype(F32)
    label_col = jnp.sum(jnp.where(at0 == at1, label_row, 0.0), axis=1, keepdims=True)
    same = label_col == label_row
    rank_row = jnp.sum(jnp.where(same & (at0 < at1), 1.0, 0.0), axis=0, keepdims=True)
    rank_col = jnp.sum(jnp.where(same & (at1 < at0), 1.0, 0.0), axis=1, keepdims=True)
    slot_row = label_row * (2 * CAP) + rank_row
    slot_ids = lax.broadcasted_iota(jnp.int32, (EXPERTS * 2 * CAP, TOK), 0).astype(F32)
    select = [(slot_ids == slot_row + half * CAP).astype(BF16) for half in range(2)]

    domain = lax.broadcasted_iota(jnp.int32, (EXPERTS, TOK), 0).astype(F32)
    lane = lax.broadcasted_iota(jnp.int32, (EXPERTS, TOK), 1)
    member = (domain == label_row).astype(F32)
    loss_sum = jnp.sum(member * losses_ref[...], axis=1, keepdims=True)
    count = jnp.sum(member, axis=1, keepdims=True)
    stat_src[0] = jnp.where(lane == 0, loss_sum, jnp.where(lane == 1, count, 0.0))

    ends = [lengths_ref[0, 0]]
    for i in range(1, 4):
        ends.append(ends[-1] + lengths_ref[0, i])
    doc0 = sum((at0 >= end).astype(jnp.int32) for end in ends)
    doc1 = sum((at1 >= end).astype(jnp.int32) for end in ends)
    allowed = (doc0 == doc1) & (at1 <= at0)
    for head in range(COLS // HEAD_DIM):
        cut = slice(head * HEAD_DIM, (head + 1) * HEAD_DIM)
        scores = lax.dot_general(
            q_v[:, cut], k_v[:, cut], NT, preferred_element_type=F32
        ) * HEAD_DIM ** (-0.5)
        scores = jnp.where(allowed, scores, -1e30)
        exp_scores = jnp.exp(scores - jnp.max(scores, axis=1, keepdims=True))
        probs = (exp_scores / jnp.sum(exp_scores, axis=1, keepdims=True)).astype(BF16)
        attn = jnp.dot(probs, v_v[:, cut], preferred_element_type=F32)
        hidden[:, cut] = (res_v[:, cut].astype(F32) + attn).astype(BF16)
    packed[...] = (
        (
            jnp.dot(select[0], hidden[:, :WIDE], preferred_element_type=F32)
            + jnp.dot(select[1], hidden[:, WIDE:], preferred_element_type=F32)
        )
        .astype(BF16)
        .reshape(EXPERTS, 2 * CAP, WIDE)
    )

    pl.semaphore_wait(barrier, len(peers))

    kind = lax.rem(x + y, 4)
    my_q = jnp.where(kind >= 2, (kind - 2) * 4 + y, 8 + y)

    def goes(ty):
        return (kind >= 2) | (lax.rem(ty, 2) == kind)

    def send_block(i):
        dx, dy = offsets[i]
        tx, ty = lax.rem(x + dx, 4), lax.rem(y + dy, 4)
        copy = remote(
            packed.at[2 * tx + ty // 2], stage.at[my_q], a_send.at[i], a_recv.at[my_q], plane(tx, ty)
        )
        return goes(ty), copy

    for i in range(15):
        allowed_i, copy = send_block(i)
        pl.when(allowed_i)(copy.start)

    @pl.when(goes(y))
    def _():
        stage[my_q] = packed[2 * x + y // 2]

    def seq_of(q):
        sy = q % 4
        if q < 8:
            return (2 + q // 4 - sy) % 4, sy
        return lax.rem(yb - sy + 4, 4), sy

    def stat_copy(i, phase):
        if phase == 0:
            dst, peer = stat_x, plane(lax.rem(x + i, 4), y)
            return remote(stat_src.at[0], dst.at[x], st_send.at[i - 1], st_recv.at[x], peer)
        if phase == 1:
            dst, peer = stat_y, plane(x, lax.rem(y + i, 4))
            return remote(stat_src.at[1], dst.at[y], st_send.at[2 + i], st_recv.at[4 + y], peer)
        return remote(stat_src.at[2], stat_c, st_send.at[6], st_recv.at[8], sibling)

    def stat_wait(i, phase):
        if phase == 0:
            at = lax.rem(x + i, 4)
            return remote(stat_src.at[0], stat_x.at[at], st_send.at[0], st_recv.at[at], plane(at, y))
        at = lax.rem(y + i, 4)
        return remote(stat_src.at[1], stat_y.at[at], st_send.at[0], st_recv.at[4 + at], plane(x, at))

    def stats(step):
        if step == 0:
            for i in range(1, 4):
                stat_copy(i, 0).start()
            stat_x[x] = stat_src[0]
        elif step == 1:
            for i in range(1, 4):
                stat_wait(i, 0).wait_recv()
            stat_src[1] = (stat_x[0] + stat_x[1]) + (stat_x[2] + stat_x[3])
            for i in range(1, 4):
                stat_copy(i, 1).start()
            stat_y[y] = stat_src[1]
        elif step == 2:
            for i in range(1, 4):
                stat_wait(i, 1).wait_recv()
            stat_src[2] = (stat_y[0] + stat_y[1]) + (stat_y[2] + stat_y[3])
            stat_copy(0, 2).start()
        else:
            stat_copy(0, 2).wait_recv()
            totals = stat_src[2] + stat_c[...]
            domain_mean = totals[:, 0:1] / totals[:, 1:2]
            eye = lax.broadcasted_iota(jnp.int32, (EXPERTS, EXPERTS), 0) == lax.broadcasted_iota(
                jnp.int32, (EXPERTS, EXPERTS), 1
            )
            mean_row = jnp.sum(jnp.where(eye, domain_mean, 0.0), axis=0, keepdims=True)
            scaled = prior_ref[...] * jnp.exp(dro_step * mean_row)
            weights_ref[...] = EXPERTS * scaled / jnp.sum(scaled, axis=1, keepdims=True)

    acc[...] = jnp.zeros_like(acc)
    square[...] = jnp.zeros_like(square)
    for i in range(16):
        @pl.when(jnp.logical_not(goes(i % 4)))
        def _():
            ret[i] = jnp.zeros((2 * CAP, WIDE), BF16)

    for load in weight_loads:
        load.wait()

    def turn(i, carry):
        at = pl.ds(pl.multiple_of(i * COLS, COLS), COLS)
        for half, source in enumerate((gate_v, up_v)):
            first = half * HALF_N
            both_v[at, first + HALF_N - 128:first + HALF_N] = jnp.zeros((COLS, 128), BF16)
            both_v[at, first:first + HID] = source[:, at].T
        return carry

    lax.fori_loop(0, NZ, turn, 0)

    own_off = SHARED + yb * CHUNK
    other_off = SHARED + (1 - yb) * CHUNK
    OWN, C0, C1, OTHER = 0, 1, 2, 3
    piece_off = (own_off, 0, CHUNK, other_off)
    b_first = 2 * SHARED
    own_at = (b_first + yb * CHUNK, 0, CHUNK, b_first + (1 - yb) * CHUNK)
    groups = {"a": (0, 0, 0), "b": (b_first, SHARED, 1)}
    lanes = {"B": (OWN, OWN), "A0": (C0, C1), "A1": (C1, C0)}
    first_q = {C0: 0, C1: 4, OWN: 8}

    def slice_at(rel):
        return lax.rem(z + rel, NZ)

    def rel_of(way, distance):
        return distance if way == RIGHT else (NZ - distance) % NZ

    def rows_at(off, rows):
        if isinstance(off, int):
            return pl.ds(off, rows)
        return pl.ds(pl.multiple_of(off, 16), rows)

    def part_of(way, lane, distance):
        if distance < 4 or lane in ("A0", "A1"):
            return 0, CHUNK
        return way * HALF, HALF

    started = []

    def go(copy):
        copy.start()
        started.append(copy)

    def gather_copy(way, hop, lane, sending):
        rel = rel_of(1 - way, hop - 1 if sending else hop)
        piece = lanes[lane][way]
        first, rows = part_of(way, lane, hop)
        ref = xb.at[slice_at(rel), rows_at(own_at[piece] + first, rows)]
        at = (way, hop - 1, piece)
        return remote(ref, ref, g_send.at[at], g_recv.at[at], toward[way])

    def sib_copy(group, rel):
        first, _, number = groups[group]
        rows = xb.at[slice_at(rel)]
        return remote(
            rows.at[pl.ds(first, SHARED)], rows.at[pl.ds(first + SHARED, SHARED)],
            gs_send.at[rel, number], gs_recv.at[rel, number], sibling,
        )

    def share(group, rel):
        go(sib_copy(group, rel))

    def y_copy(rel, mine=True):
        ref = xb.at[slice_at(rel), rows_at(own_at[OWN if mine else OTHER], CHUNK)]
        return remote(ref, ref, gy_send.at[rel], gy_recv.at[rel], partner)

    def spread(rel, piece):
        if piece == OWN:
            go(y_copy(rel))

    def start(piece):
        first = first_q[piece]
        for q in range(first, first + 4):
            sx, sy = seq_of(q)
            arrival = remote(
                packed.at[0], stage.at[q], a_send.at[0], a_recv.at[q], plane(sx, sy)
            )
            pl.when((sx != x) | (sy != y))(arrival.wait_recv)
        blocks = stage[first:first + 4].astype(F32)
        here = rows_at(own_at[piece], CHUNK)
        for half in range(2):
            xb[z, here, half * WIDE:(half + 1) * WIDE] = (
                blocks[:, half * CAP:(half + 1) * CAP].reshape(CHUNK, WIDE).astype(BF16)
            )

    def first_hop(lane):
        for way in (RIGHT, LEFT):
            go(gather_copy(way, 1, lane, True))

    def own_spread(piece):
        spread(0, piece)

    def hop(lane, h):
        for way in (RIGHT, LEFT):
            gather_copy(way, h, lane, False).wait_recv()
            if h < 3 or (h == 3 and lane != "A1"):
                go(gather_copy(way, h + 1, lane, True))
        first, second = lanes[lane]
        if h == 4 and first == second:
            spread(4, first)
            return
        for way in (RIGHT, LEFT):
            spread(rel_of(1 - way, h), lanes[lane][way])

    def y_arrive(*rels):
        for rel in rels:
            y_copy(rel, mine=False).wait_recv()
            share("b", rel)

    def multiply(group, *rels):
        here = pl.ds(groups[group][0], 2 * SHARED)
        for rel in rels:
            sib_copy(group, rel).wait_recv()
            s = slice_at(rel)
            at = pl.ds(pl.multiple_of(s * COLS, COLS), COLS)
            value = xb[s, here, :].astype(F32)
            sq = value * value
            square[here, :] += sq[:, :128] + sq[:, 128:256] + sq[:, 256:384] + sq[:, 384:]
            scaled = (value * gain_ref[:, at]).astype(BF16)
            acc[here, :] += jnp.dot(scaled, both_v[at, :], preferred_element_type=F32)

    def activate(group):
        here = pl.ds(groups[group][0], 2 * SHARED)
        mean = jnp.sum(square[here, :], axis=1, keepdims=True) * (1.0 / (NZ * COLS))
        scale = lax.rsqrt(mean + 1e-05)
        gate = acc[here, :HID] * scale
        up = acc[here, HALF_N:HALF_N + HID] * scale
        inner[here, :] = (gate / (1.0 + jnp.exp(-gate)) * up).astype(BF16)

    def rs_copy(group, rel):
        _, off, number = groups[group]
        here = pl.ds(off, SHARED)
        at = (rel, number)
        return remote(
            sib_out.at[rel, here], sib_in.at[rel, here], rs_send.at[at], rs_recv.at[at], sibling
        )

    def ry_copy(rel):
        return remote(y_out.at[rel], y_in.at[rel], ry_send.at[rel], ry_recv.at[rel], partner)

    def prepare(group, *rels):
        first, off, _ = groups[group]
        for rel in rels:
            value = jnp.dot(
                inner[first:first + 2 * SHARED, :], down_v[slice_at(rel)], preferred_element_type=F32
            )
            sib_out[rel, off:off + SHARED] = value[SHARED:].astype(BF16)
            part[rel, off:off + SHARED] = value[:SHARED]
            go(rs_copy(group, rel))

    def join(group, *rels):
        for rel in rels:
            rs_copy(group, rel).wait_recv()
            if group == "a":
                part[rel, :SHARED] += sib_in[rel, :SHARED].astype(F32)
                continue
            other = rows_at(other_off, CHUNK)
            y_out[rel] = (part[rel, other] + sib_in[rel, other].astype(F32)).astype(BF16)
            go(ry_copy(rel))
            own = rows_at(own_off, CHUNK)
            part[rel, own] += sib_in[rel, own].astype(F32)

    def y_join(*rels):
        own = rows_at(own_off, CHUNK)
        for rel in rels:
            ry_copy(rel).wait_recv()
            part[rel, own] += y_in[rel].astype(F32)

    def ring_copy(way, distance, lane):
        piece = lanes[lane][way]
        first, rows = part_of(way, lane, distance)
        here = rows_at(piece_off[piece] + first, rows)
        at = (way, distance - 1, piece)
        return remote(
            ring_out.at[way, distance - 1, here], ring_in.at[way, distance - 1, here],
            r_send.at[at], r_recv.at[at], toward[way],
        )

    def incoming(way, distance, lane):
        ring_copy(way, distance, lane).wait_recv()
        first, rows = part_of(way, lane, distance)
        here = rows_at(piece_off[lanes[lane][way]] + first, rows)
        return ring_in[way, distance - 1, here].astype(F32)

    def ring(lane, distance):
        for way in (RIGHT, LEFT):
            first, rows = part_of(way, lane, distance)
            here = rows_at(piece_off[lanes[lane][way]] + first, rows)
            value = part[rel_of(way, distance), here]
            if distance < 3 or (distance == 3 and lane == "A0"):
                value = value + incoming(way, distance + 1, lane)
            elif distance == 3 and lane != "A1":
                arrived = incoming(way, 4, lane)
                if way == RIGHT:
                    value = jnp.concatenate([value[:HALF] + arrived, value[HALF:]], axis=0)
                else:
                    value = jnp.concatenate([value[:HALF], value[HALF:] + arrived], axis=0)
            ring_out[way, distance - 1, here] = value.astype(BF16)
            go(ring_copy(way, distance, lane))

    def send_back(q):
        sx, sy = seq_of(q)
        return remote(ret_out.at[q], ret.at[xy], b_send.at[q], b_recv.at[xy], plane(sx, sy))

    def is_me(q):
        sx, sy = seq_of(q)
        return (sx == x) & (sy == y)

    def finish(piece):
        value = part[0, rows_at(piece_off[piece], CHUNK)]
        for way in (RIGHT, LEFT):
            lane = next(name for name in used if lanes[name][way] == piece)
            value = value + incoming(way, 1, lane)
        first = first_q[piece]
        ret_out[first:first + 4] = jnp.concatenate(
            [value[:, :WIDE].reshape(4, CAP, WIDE), value[:, WIDE:].reshape(4, CAP, WIDE)], axis=1
        ).astype(BF16)
        for q in range(first, first + 4):
            pl.when(jnp.logical_not(is_me(q)))(send_back(q).start)

    def retire(count):
        for copy in started[:count]:
            copy.wait_send()
        del started[:count]

    used = ("B", "A0", "A1")
    start(OWN)
    spread(0, OWN)
    first_hop("B")
    start(C0)
    spread(0, C0)
    start(C1)
    spread(0, C1)
    first_hop("A0")
    share("a", 0)
    first_hop("A1")
    multiply("a", 0)
    y_arrive(0)
    hop("B", 1)
    stats(0)
    multiply("b", 0)
    hop("A0", 1)
    hop("A1", 1)
    share("a", 1)
    share("a", 7)
    multiply("a", 1)
    hop("B", 2)
    stats(1)
    multiply("a", 7)
    y_arrive(1, 7)
    hop("A0", 2)
    multiply("b", 1)
    multiply("b", 7)
    hop("A1", 2)
    share("a", 2)
    share("a", 6)
    multiply("a", 2)
    hop("B", 3)
    multiply("a", 6)
    y_arrive(2, 6)
    hop("A0", 3)
    multiply("b", 2)
    multiply("b", 6)
    hop("A1", 3)
    share("a", 5)
    share("a", 3)
    hop("B", 4)
    stats(2)
    multiply("a", 5)
    multiply("a", 3)
    hop("A0", 4)
    share("a", 4)
    y_arrive(3, 5)
    multiply("a", 4)
    activate("a")
    prepare("a", 3)
    y_arrive(4)
    prepare("a", 4)
    multiply("b", 3)
    multiply("b", 5)
    multiply("b", 4)
    activate("b")
    prepare("b", 4)
    prepare("b", 6)
    join("a", 3)
    prepare("b", 3)
    join("a", 4)
    join("b", 4)
    ring("A0", 4)
    prepare("a", 5)
    join("b", 3)
    prepare("a", 7)
    prepare("b", 5)
    join("a", 5)
    ring("A1", 3)
    prepare("a", 6)
    join("a", 7)
    join("b", 5)
    prepare("a", 2)
    join("b", 6)
    y_join(4)
    ring("B", 4)
    retire(12)
    ring("A0", 3)
    retire(12)
    join("a", 2)
    prepare("b", 7)
    prepare("b", 2)
    prepare("a", 0)
    join("a", 6)
    ring("A1", 2)
    retire(12)
    join("b", 7)
    join("b", 2)
    y_join(5)
    join("a", 0)
    y_join(3)
    ring("B", 3)
    retire(12)
    prepare("a", 1)
    prepare("b", 0)
    y_join(6)
    prepare("b", 1)
    ring("A0", 2)
    retire(12)
    join("a", 1)
    join("b", 0)
    join("b", 1)
    ring("A1", 1)
    for i in range(15):
        allowed_i, copy = send_block(i)
        pl.when(allowed_i)(copy.wait_send)
    for i in range(1, 4):
        stat_copy(i, 0).wait_send()
        stat_copy(i, 1).wait_send()
    stat_copy(0, 2).wait_send()
    y_join(7)
    y_join(2)
    ring("B", 2)
    retire(16)
    ring("A0", 1)
    retire(8)
    y_join(0)
    y_join(1)
    ring("B", 1)
    stats(3)
    finish(C1)
    finish(C0)
    finish(OWN)

    @pl.when(goes(y))
    def _():
        ret[xy] = ret_out[my_q]

    retire(len(started))

    place = lax.broadcasted_iota(jnp.int32, (TOK, 16 * 2 * CAP), 1).astype(F32)
    spot = label_col * (4 * CAP) + rank_col
    take = [
        ((place == spot + half * CAP) | (place == spot + (2 + half) * CAP)).astype(BF16)
        for half in range(2)
    ]
    for i in range(16):
        arrival = remote(
            ret_out.at[0], ret.at[i], b_send.at[0], b_recv.at[i], plane(i // 4, i % 4)
        )
        pl.when(goes(i % 4) & (xy != i))(arrival.wait_recv)
    returned = ret[...].reshape(16 * 2 * CAP, WIDE)
    for half in range(2):
        cut = slice(half * WIDE, (half + 1) * WIDE)
        expert_out = jnp.dot(take[half], returned, preferred_element_type=F32)
        mixed_ref[:, cut] = (hidden[:, cut].astype(F32) + expert_out).astype(BF16)
    for q in range(12):
        pl.when(jnp.logical_not(is_me(q)))(send_back(q).wait_send)


def hand_on(mixed_in, weights_in, mixed_out, weights_out):
    mixed_out[...] = mixed_in[...]
    weights_out[...] = weights_in[...]


def body(
    residual, queries, key_rows, value_rows, lengths, labels, losses, prior_weights, norm_gain,
    gate_weight, up_weight, down_weight,
):
    vmem = pl.BlockSpec(memory_space=pltpu.VMEM)
    hbm = pl.BlockSpec(memory_space=pl.ANY)
    dma = pltpu.SemaphoreType.DMA
    tile = (TOK, COLS)
    mixed, weights = pl.pallas_call(
        kernel,
        out_shape=(
            jax.ShapeDtypeStruct(tile, BF16),
            jax.ShapeDtypeStruct((1, EXPERTS), F32),
        ),
        in_specs=[hbm] * 12,
        out_specs=(vmem, vmem),
        scratch_shapes=[
            pltpu.SMEM((1, 4), jnp.int32),
            pltpu.VMEM((1, TOK), jnp.int32),
            pltpu.VMEM((1, TOK), F32),
            pltpu.VMEM((1, EXPERTS), F32),
            pltpu.VMEM((1, NZ * COLS), F32),
            pltpu.VMEM(tile, BF16),
            pltpu.VMEM(tile, BF16),
            pltpu.VMEM(tile, BF16),
            pltpu.VMEM(tile, BF16),
            pltpu.VMEM((HID, NZ * COLS), BF16),
            pltpu.VMEM((HID, NZ * COLS), BF16),
            pltpu.VMEM((NZ, HID, COLS), BF16),
            pltpu.VMEM((NZ * COLS, 2 * HALF_N), BF16),
            pltpu.VMEM(tile, BF16),
            pltpu.VMEM((EXPERTS, 2 * CAP, WIDE), BF16),
            pltpu.VMEM((12, 2 * CAP, WIDE), BF16),
            pltpu.VMEM((NZ, ROWS, COLS), BF16),
            pltpu.VMEM((ROWS, 2 * HALF_N), F32),
            pltpu.VMEM((ROWS, 128), F32),
            pltpu.VMEM((ROWS, HID), BF16),
            pltpu.VMEM((NZ, CORE_ROWS, COLS), F32),
            pltpu.VMEM((NZ, CORE_ROWS, COLS), BF16),
            pltpu.VMEM((NZ, CORE_ROWS, COLS), BF16),
            pltpu.VMEM((2, 4, CORE_ROWS, COLS), BF16),
            pltpu.VMEM((2, 4, CORE_ROWS, COLS), BF16),
            pltpu.VMEM((NZ, CHUNK, COLS), BF16),
            pltpu.VMEM((NZ, CHUNK, COLS), BF16),
            pltpu.VMEM((12, 2 * CAP, WIDE), BF16),
            pltpu.VMEM((16, 2 * CAP, WIDE), BF16),
            pltpu.VMEM((4, EXPERTS, 128), F32),
            pltpu.VMEM((4, EXPERTS, 128), F32),
            pltpu.VMEM((EXPERTS, 128), F32),
            pltpu.VMEM((3, EXPERTS, 128), F32),
            dma((9,)), dma((2 + NZ,)),
            dma((15,)), dma((12,)),
            dma((2, 4, 3)), dma((2, 4, 3)),
            dma((NZ, 2)), dma((NZ, 2)),
            dma((NZ,)), dma((NZ,)),
            dma((NZ, 2)), dma((NZ, 2)),
            dma((NZ,)), dma((NZ,)),
            dma((2, 4, 3)), dma((2, 4, 3)),
            dma((12,)), dma((16,)),
            dma((7,)), dma((9,)),
        ],
        compiler_params=pltpu.CompilerParams(
            collective_id=0, has_side_effects=True, vmem_limit_bytes=60 * 1024 * 1024
        ),
    )(
        lengths, labels.reshape(1, TOK), losses.reshape(1, TOK), prior_weights.reshape(1, EXPERTS),
        norm_gain.reshape(1, NZ * COLS), residual, queries, key_rows, value_rows,
        gate_weight.T, up_weight.T, down_weight,
    )
    mixed, weights = pl.pallas_call(
        hand_on,
        out_shape=(
            jax.ShapeDtypeStruct(tile, BF16),
            jax.ShapeDtypeStruct((1, EXPERTS), F32),
        ),
        in_specs=[vmem, vmem],
        out_specs=(vmem, vmem),
    )(mixed, weights)
    return (mixed, weights.reshape(EXPERTS))


def solution(mesh):
    placed = (
        P("dp", "mp"),
        P("dp", "mp"),
        P("dp", "mp"),
        P("dp", "mp"),
        P("dp", None),
        P("dp", None),
        P("dp"),
        P(),
        P(),
        P(None, ("dp", "mp")),
        P(None, ("dp", "mp")),
        P(("dp", "mp"), None),
    )
    return jax.shard_map(
        body, mesh=mesh, in_specs=placed, out_specs=(P("dp", "mp"), P()), check_vma=False
    )
```
